256 devices in a mesh: section: 4 (over y_lo, core), batch: 16 (over z, y_hi), mp: 4 (over x).
Axes of the slice: x: 4, y: 4 (y_hi: 2, y_lo: 2; y = y_hi * 2 + y_lo), z: 8, core: 2. Of those that a mesh axis runs over, the one named last changes fastest.
Arguments:
- hidden_in: bfloat16 [1024, 8, 4096], P('batch'), may hold values from -6 to 6
- model_tokens: int32 [1024, 8, 8], P(('batch', 'section')), may hold values from 0 to 2047
- user_tokens: int32 [1024, 8, 8], P(('batch', 'section')), may hold values from 0 to 2047
- codebooks: bfloat16 [8, 2048, 256], P(None, 'batch'), may hold values from -2 to 2
- decode_proj: bfloat16 [256, 512], P(None, 'mp'), may hold values from -0.375 to 0.375
- conv_weight: bfloat16 [4, 3, 512, 512], P(None, None, None, 'mp'), may hold values from -0.21875 to 0.21875
- conv_state: bfloat16 [1024, 4, 2, 512], P(('batch', 'section')), may hold values from -0.8984375 to 2
- user_proj: bfloat16 [256, 4096], P(None, ('section', 'mp')), may hold values from -0.375 to 0.375
- norm_gain: bfloat16 [4096], replicated, may hold values from 0.5 to 1.5
- w_qkv: bfloat16 [4096, 3, 4096], P(None, None, ('section', 'mp')), as said below
- w_out: bfloat16 [4096, 4096], P(('section', 'mp')), may hold values from -0.375 to 0.375
- kv_cache: bfloat16 [2, 1024, 32, 64, 128], P(None, 'batch', ('section', 'mp')), may hold values from -6 to 6
- cache_len: int32 [1024], P('batch'), may hold values from 0 to 64, as said below
Outputs:
- layer_out: bfloat16 [1024, 8, 4096], P('batch')
- decoded: bfloat16 [1024, 8, 512], P(('batch', 'section'), None, 'mp')
The draws below stay inside these ranges and needn't reach their ends.
Inputs may be any that keep to these rules, and one draw needn't show every extreme that they name: `cache_len`: a dialogue holds at most 64 earlier frames, and some dialogue holds exactly 64. `w_qkv`: every entry lies within 6 / sqrt(4096) of zero.
All inputs are finite; a program needn't handle non-finite values.
Results may differ from the reference program's by a relative error of at most 0.02.
Values may be sent and summed in bfloat16 or wider, within the bound.
A program may use at most 128 MiB of HBM per device.

```python
import jax
import jax.numpy as jnp
from jax import lax

D = 4096
HEADS = 32
HD = 128
CB = 8
CARD = 2048
CD = 256
CH = 512
KER = 3
LAYERS_C = 4
FRAMES = 8
CACHE = 64
DIAL = 1024
N_SECTION = 4
N_MP = 4


def draw_hidden_in(key, part):
    salted = jax.random.fold_in(key, 21)
    values = jax.random.truncated_normal(salted, -6.0, 6.0, (DIAL, FRAMES, D), jnp.float32)
    return values.astype(jnp.bfloat16)


def draw_w_qkv(key, part):
    salted = jax.random.fold_in(key, 22)
    scale = D ** (-0.5)
    weights = jax.random.truncated_normal(salted, -6.0, 6.0, (D, 3, HEADS, HD), jnp.float32) * scale
    return weights.reshape(D, 3, HEADS * HD).astype(jnp.bfloat16)


def draw_kv_cache(key, part):
    salted = jax.random.fold_in(key, 23)
    cache = jax.random.truncated_normal(salted, -6.0, 6.0, (2, DIAL, HEADS, CACHE, HD), jnp.float32)
    return cache.astype(jnp.bfloat16)


def draw_cache_len(key, part):
    key = jax.random.fold_in(key, 11)
    first, second = jax.random.split(key)
    lengths = jax.random.randint(first, (DIAL,), 0, CACHE + 1)
    place = jax.random.randint(second, (), 0, DIAL)
    return jnp.where(jnp.arange(DIAL) == place, CACHE, lengths).astype(jnp.int32)


def touch_ends(entries, stream_key, smallest, largest):
    dims = entries.shape
    spot = [jax.random.randint(jax.random.fold_in(stream_key, axis), (), 0, dims[axis]) for axis in range(len(dims))]
    entries = entries.at[tuple(spot)].set(smallest)
    longest = dims.index(max(dims))
    spot[longest] = (spot[longest] + 1) % dims[longest]
    return entries.at[tuple(spot)].set(largest)


def level_of(own_key, extent, cuts, low, high):
    level, own = 1.0, jax.random.fold_in(own_key, 6)
    for axis_at, parts in cuts:
        draws = jnp.exp(jax.random.uniform(jax.random.fold_in(own, axis_at), (parts,), jnp.float32, low / len(cuts), high / len(cuts)))
        level = level * jnp.repeat(draws, extent[axis_at] // parts).reshape([-1 if axis == axis_at else 1 for axis in range(len(extent))])
    return level


def bell_draw(stream_key, shape, scale, bound, cuts=(), kind=jnp.bfloat16):
    values = scale * jax.random.normal(stream_key, shape, jnp.float32)
    if cuts:
        values = values * level_of(stream_key, shape, cuts, -0.22, 0.18)
    return jnp.clip(values, -bound, bound).astype(kind)


def setup_inputs(seed: int = 0) -> dict:
    splits = jax.random.split(jax.random.key(seed), 14)
    return {
        "hidden_in": draw_hidden_in(jax.random.fold_in(splits[13], 71), 0),
        "model_tokens": touch_ends(jax.random.randint(splits[1], (DIAL, FRAMES, CB), 0, CARD), jax.random.fold_in(splits[1], 1), 0, CARD - 1).astype(jnp.int32),
        "user_tokens": touch_ends(jax.random.randint(splits[2], (DIAL, FRAMES, CB), 0, CARD), jax.random.fold_in(splits[2], 1), 0, CARD - 1).astype(jnp.int32),
        "codebooks": bell_draw(splits[3], (CB, CARD, CD), 0.35, 2.0, ((1, 16),)),
        "decode_proj": bell_draw(splits[4], (CD, CH), CD ** -0.5, 0.375, ((1, 4),)),
        "conv_weight": bell_draw(splits[5], (LAYERS_C, KER, CH, CH), (KER * CH // 2) ** -0.5, 0.21875, ((3, 4),)),
        "conv_state": jnp.clip(-0.8984375 + 2.8984375 * jax.random.uniform(splits[6], (DIAL, LAYERS_C, KER - 1, CH), jnp.float32) ** level_of(splits[6], (DIAL, LAYERS_C, KER - 1, CH), ((0, 64),), -0.2, 0.2), -0.8984375, 2.0).astype(jnp.bfloat16),
        "user_proj": bell_draw(splits[7], (CD, D), CD ** -0.5, 0.375, ((1, 16),)),
        "norm_gain": jnp.clip(1.0 + 0.1 * jax.random.normal(splits[8], (D,), jnp.float32), 0.5, 1.5).astype(jnp.bfloat16),
        "w_qkv": draw_w_qkv(jax.random.fold_in(splits[13], 71), 0),
        "w_out": bell_draw(splits[10], (HEADS * HD, D), (HEADS * HD // 16) ** -0.5, 0.375, ((0, 16),)),
        "kv_cache": draw_kv_cache(jax.random.fold_in(splits[13], 71), 0),
        "cache_len": draw_cache_len(jax.random.fold_in(splits[13], 71), 0),
    }


def rotate(x, pos):
    half = x.shape[-1] // 2
    freq = 10000.0 ** (-(jnp.arange(half, dtype=jnp.float32) * 2.0 / x.shape[-1]))
    angle = pos[..., None] * freq
    cosine = jnp.cos(angle)[..., None, :]
    sine = jnp.sin(angle)[..., None, :]
    first = x[..., :half]
    second = x[..., half:]
    return jnp.concatenate([first * cosine - second * sine, first * sine + second * cosine], axis=-1)

def reference(hidden_in, model_tokens, user_tokens, codebooks, decode_proj, conv_weight, conv_state, user_proj, norm_gain, w_qkv, w_out, kv_cache, cache_len):
    books = codebooks.astype(jnp.float32)
    index_cb = jnp.arange(CB)
    latent_model = lax.optimization_barrier(jnp.sum(books[index_cb, model_tokens], axis=2)).astype(jnp.bfloat16)
    latent_user = lax.optimization_barrier(jnp.sum(books[index_cb, user_tokens], axis=2)).astype(jnp.bfloat16)
    user_emb = jnp.dot(latent_user.reshape(-1, CD), user_proj, preferred_element_type=jnp.float32).astype(jnp.bfloat16)
    x0 = hidden_in.astype(jnp.float32) + user_emb.reshape(DIAL, FRAMES, D).astype(jnp.float32)
    meansq = lax.optimization_barrier(jnp.mean(x0 * x0, axis=-1, keepdims=True))
    xn = (x0 * lax.rsqrt(meansq + 1e-05) * norm_gain.astype(jnp.float32)).astype(jnp.bfloat16)
    qkv = jnp.dot(xn.reshape(-1, D), w_qkv.reshape(D, -1), preferred_element_type=jnp.float32)
    qkv = qkv.reshape(DIAL, FRAMES, 3, HEADS, HD)
    pos = (cache_len[:, None] + jnp.arange(FRAMES, dtype=jnp.int32)[None, :]).astype(jnp.float32)
    query = rotate(qkv[:, :, 0], pos).astype(jnp.bfloat16).astype(jnp.float32)
    key_new = rotate(qkv[:, :, 1], pos).astype(jnp.bfloat16).astype(jnp.float32)
    value_new = qkv[:, :, 2].astype(jnp.bfloat16).astype(jnp.float32)
    cache_k = kv_cache[0].astype(jnp.float32)
    cache_v = kv_cache[1].astype(jnp.float32)
    scale = 1.0 / HD ** 0.5
    old_scores = jnp.einsum('bfhe,bhce->bhfc', query, cache_k) * scale
    valid = (jnp.arange(CACHE, dtype=jnp.int32)[None, :] < cache_len[:, None])[:, None, None, :]
    old_scores = jnp.where(valid, old_scores, -1e+30)
    new_scores = jnp.einsum('bfhe,bghe->bhfg', query, key_new) * scale
    causal = jnp.arange(FRAMES)[None, :] <= jnp.arange(FRAMES)[:, None]
    new_scores = jnp.where(causal[None, None], new_scores, -1e+30)
    scores = jnp.concatenate([old_scores, new_scores], axis=-1)
    top = lax.optimization_barrier(jnp.max(scores, axis=-1, keepdims=True))
    expo = jnp.exp(scores - top)
    probs = (expo / lax.optimization_barrier(jnp.sum(expo, axis=-1, keepdims=True))).astype(jnp.bfloat16).astype(jnp.float32)
    attn = jnp.einsum('bhfc,bhce->bfhe', probs[..., :CACHE], cache_v) + jnp.einsum('bhfg,bghe->bfhe', probs[..., CACHE:], value_new)
    attn = attn.astype(jnp.bfloat16).reshape(-1, HEADS * HD)
    head_groups = N_SECTION * N_MP
    group_width = HEADS * HD // head_groups
    proj = jnp.zeros((DIAL * FRAMES, D), jnp.float32)
    for head_group in range(head_groups):
        lower = head_group * group_width
        partial_sum = jnp.dot(attn[:, lower:lower + group_width], w_out[lower:lower + group_width], preferred_element_type=jnp.float32)
        proj = proj + lax.optimization_barrier(partial_sum.astype(jnp.bfloat16)).astype(jnp.float32)
    proj = proj.reshape(DIAL, FRAMES, D)
    layer_out = (x0 + proj).astype(jnp.bfloat16)
    state = jnp.dot(latent_model.reshape(-1, CD), decode_proj, preferred_element_type=jnp.float32).reshape(DIAL, FRAMES, CH)
    for layer in range(LAYERS_C):
        excited = jax.nn.elu(state).astype(jnp.bfloat16)
        padded = jnp.concatenate([conv_state[:, layer], excited], axis=1)
        total = state
        for tap in range(KER):
            window = padded[:, tap:tap + FRAMES].reshape(-1, CH)
            total = total + jnp.dot(window, conv_weight[layer, tap], preferred_element_type=jnp.float32).reshape(DIAL, FRAMES, CH)
        state = total
    decoded = state.astype(jnp.bfloat16)
    return (layer_out, decoded)
```

```python
import functools
import math

import jax
import jax.numpy as jnp
from jax import lax
from jax.experimental import pallas as pl
from jax.experimental.pallas import tpu as pltpu
from jax.sharding import PartitionSpec as P

F32 = jnp.float32
BF16 = jnp.bfloat16
MESH = pl.DeviceIdType.MESH

NS, NB, NM = 4, 16, 4
NG = NS * NM
ROWS = 512
WIDTH = 4096
NCHUNK = 4
CROWS = ROWS // NCHUNK
NEG = -1e30


def dot(a, b):
    return jnp.dot(a, b, preferred_element_type=F32)


def dot_t(a, b):
    return lax.dot_general(a, b, (((1,), (1,)), ((), ())), preferred_element_type=F32)


class Sems:
    def __init__(self, ref):
        self.ref = ref
        self.used = 0

    def take(self, count=1):
        first = self.used
        self.used += count
        return first


def kernel(
    h_hbm,
    mt_hbm,
    ut_hbm,
    cb_hbm,
    dp_hbm,
    cw_hbm,
    cs_hbm,
    up_hbm,
    g_hbm,
    w_hbm,
    wo_hbm,
    kv_hbm,
    len_ref,
    out_hbm,
    dec_hbm,
    h_v,
    tok_v,
    cb_v,
    dp_v,
    cw_v,
    el_v,
    g_v,
    w_v,
    wo_v,
    kv_v,
    upg,
    tsend,
    trecv,
    oh_u,
    oh_m,
    part_u,
    part_m,
    recv_u,
    recv_m,
    lg,
    lmg,
    lu,
    mq,
    mqb,
    acc,
    ss,
    cos_v,
    sin_v,
    attn_g,
    psend,
    precv,
    outv,
    decv,
    lsem,
    ssem,
    rsem,
):
    s = lax.axis_index("section")
    b = lax.axis_index("batch")
    m = lax.axis_index("mp")
    me = s * NM + m
    c1 = s + 1 - 2 * lax.rem(s, 2)
    y1 = lax.rem(s + 2, NS)
    xp = lax.rem(m + 1, NM)
    xm = lax.rem(m + NM - 1, NM)
    xd = lax.rem(m + 2, NM)

    local = Sems(lsem)
    remote = Sems(ssem)
    sends = []

    def load(src, dst):
        copy = pltpu.make_async_copy(src, dst, lsem.at[local.take()])
        copy.start()
        return copy

    def send(src, dst, ds=None, db=None, dm=None):
        at = remote.take()
        copy = pltpu.make_async_remote_copy(
            src_ref=src,
            dst_ref=dst,
            send_sem=ssem.at[at],
            recv_sem=rsem.at[at],
            device_id=(
                s if ds is None else ds,
                b if db is None else db,
                m if dm is None else dm,
            ),
            device_id_type=MESH,
        )
        copy.start()
        sends.append(copy)
        return copy

    def spread(src, dst, axis):
        base = remote.take(15)

        def make(k):
            if axis == "batch":
                target = lax.rem(b + k, NB)
                device = (s, target, m)
            else:
                target = lax.rem(me + k, NG)
                device = (target // NM, b, lax.rem(target, NM))
            return pltpu.make_async_remote_copy(
                src_ref=src(target),
                dst_ref=dst,
                send_sem=ssem.at[base + k - 1],
                recv_sem=rsem.at[base + k - 1],
                device_id=device,
                device_id_type=MESH,
            )

        @pl.loop(1, 16)
        def _(k):
            make(k).start()

        def wait_recv():
            @pl.loop(1, 16)
            def _(k):
                make(k).wait_recv()

        def wait_send():
            @pl.loop(1, 16)
            def _(k):
                make(k).wait_send()

        return wait_recv, wait_send

    l_ut = load(ut_hbm, tok_v.at[0])
    l_mt = load(mt_hbm, tok_v.at[1])
    l_g = load(g_hbm, g_v)
    l_cb = load(cb_hbm, cb_v)
    l_up = load(up_hbm, upg.at[me])
    l_h, l_w = [], []
    for part in range(4):
        cols = pl.ds(part * 1024, 1024)
        l_h.append(load(h_hbm.at[:, cols], h_v.at[:, cols]))
        l_w.append(load(w_hbm.at[:, cols], w_v.at[:, cols]))
    l_kv = load(kv_hbm, kv_v)
    own_cols = pl.ds(pl.multiple_of(s * 1024, 1024), 1024)
    l_wo = load(wo_hbm.at[:, own_cols], wo_v.at[s])
    l_dp = load(dp_hbm, dp_v)
    l_cw = load(cw_hbm, cw_v)
    l_cs = load(cs_hbm, el_v.at[:, pl.ds(0, 32)])

    barrier = pltpu.get_barrier_semaphore()

    @pl.loop(1, 16)
    def _(k):
        pl.semaphore_signal(
            barrier, inc=1, device_id=(s, lax.rem(b + k, NB), m), device_id_type=MESH
        )
        other = lax.rem(me + k, NG)
        pl.semaphore_signal(
            barrier, inc=1, device_id=(other // NM, b, lax.rem(other, NM)), device_id_type=MESH
        )

    pl.semaphore_wait(barrier, 30)

    l_ut.wait()
    l_mt.wait()
    f0 = 2 * m
    tile = jnp.concatenate(
        [
            tok_v[0, f0],
            tok_v[0, f0 + 1],
            tok_v[1, f0],
            tok_v[1, f0 + 1],
            jnp.zeros((8, 64), jnp.int32),
        ],
        axis=1,
    )
    tsend[...] = tile
    trecv[b] = tile
    tok_wait, tok_done = spread(lambda t: tsend, trecv.at[b], "batch")

    def up_block(block):
        return upg.at[block]

    l_up.wait()
    u_y = send(up_block(me), up_block(me), ds=y1)
    u_x = [send(up_block(me), up_block(me), dm=t) for t in (xp, xm, xd)]
    wo_copies = []
    for off in (1, 2, 3):
        if off == 1:
            target = c1
        elif off == 2:
            target = y1
        else:
            target = 3 - s
        cols = pl.ds(pl.multiple_of(target * 1024, 1024), 1024)
        wo_copies.append(send(wo_hbm.at[:, cols], wo_v.at[s], ds=target))

    l_g.wait()
    acc[...] = jnp.zeros_like(acc)

    def hidden_step(step):
        cols = pl.ds(pl.multiple_of(step * 512, 512), 512)
        scaled = (h_v[:, cols].astype(F32) * g_v[:, cols]).astype(BF16)
        for j in range(3):
            acc[j] += dot(scaled, w_v[j, cols, :])

    for part in range(2):
        l_h[part].wait()
        l_w[part].wait()
        pl.loop(2 * part, 2 * part + 2)(hidden_step)

    u_y.wait_recv()
    yblk = y1 * NM + m
    u_yx = [send(up_block(yblk), up_block(yblk), dm=t) for t in (xp, xm, xd)]

    tok_wait()
    l_cb.wait()
    entry = lax.broadcasted_iota(jnp.int32, (64, 128), 1) + 128 * b

    @pl.loop(0, NB)
    def _(i):
        rows = trecv[i].T[:64]
        start = pl.multiple_of(i * 32, 32)
        for c in range(8):
            hot = jnp.where(rows[:, c : c + 1] == entry, 1.0, 0.0).astype(BF16)
            oh_u[pl.ds(start, 32), pl.ds(c * 128, 128)] = hot[:32]
            oh_m[pl.ds(start, 32), pl.ds(c * 128, 128)] = hot[32:]

    part_u[...] = dot(oh_u[...], cb_v[...]).astype(BF16).reshape(NB, 32, 256)
    pu_wait, pu_done = spread(lambda t: part_u.at[t], recv_u.at[b], "batch")
    part_m[...] = dot(oh_m[...], cb_v[...]).astype(BF16).reshape(NB, 32, 256)
    pm_wait, pm_done = spread(lambda t: part_m.at[t], recv_m.at[b], "batch")
    recv_u[b] = part_u[b]
    recv_m[b] = part_m[b]

    for part in range(2, 4):
        l_h[part].wait()
        l_w[part].wait()
        pl.loop(2 * part, 2 * part + 2)(hidden_step)

    for copy in u_x + u_yx:
        copy.wait_recv()
    mine = pl.ds(pl.multiple_of(s * NM, NM), NM)
    yours = pl.ds(pl.multiple_of(y1 * NM, NM), NM)
    u_f0 = send(upg.at[mine], upg.at[mine], ds=c1)
    u_f1 = send(upg.at[yours], upg.at[yours], ds=c1)

    def total_of(ref):
        total = ref[0].astype(F32)
        for i in range(1, NB):
            total = total + ref[i].astype(F32)
        return total.astype(BF16)

    pu_wait()
    lg[me] = total_of(recv_u)
    lg_wait, lg_done = spread(lambda t: lg.at[me], lg.at[me], "group")

    lane = lax.broadcasted_iota(jnp.int32, (64, 128), 1)
    freq = jnp.exp(lax.rem(lane, 64).astype(F32) * (-2.0 * math.log(10000.0) / 128.0))
    frame = lax.rem(lax.broadcasted_iota(jnp.int32, (64, 128), 0), 8)

    @pl.loop(0, 8)
    def _(i):
        where = lax.broadcasted_iota(jnp.int32, (64, 128), 0) // 8
        pos = frame
        for d in range(8):
            pos = pos + jnp.where(where == d, len_ref[i * 8 + d], 0)
        angle = pos.astype(F32) * freq
        rows = pl.ds(pl.multiple_of(i * 64, 64), 64)
        cos_v[rows] = jnp.cos(angle)
        sine = jnp.sin(angle)
        sin_v[rows] = jnp.where(lane < 64, -sine, sine)

    pm_wait()
    lmg[m] = total_of(recv_m)
    lm_copies = [send(lmg.at[m], lmg.at[m], dm=t) for t in (xp, xm, xd)]

    mq[...] = jnp.zeros_like(mq)
    u_f0.wait_recv()
    u_f1.wait_recv()

    @pl.loop(0, NG)
    def _(j):
        cols = pl.ds(pl.multiple_of(j * 256, 256), 256)
        scaled = (upg[j].astype(F32) * g_v[:, cols]).astype(BF16)
        for t in range(3):
            mq[t] += dot(scaled, w_v[t, cols, :])

    mqb[...] = mq[...].astype(BF16)

    lg_wait()
    to = lax.broadcasted_iota(jnp.int32, (128, 128), 0)
    frm = lax.broadcasted_iota(jnp.int32, (128, 128), 1)
    perm = jnp.where(frm == lax.rem(to, 8) * 16 + to // 8, 1.0, 0.0).astype(BF16)
    perm_back = jnp.where(frm == lax.rem(to, 16) * 8 + to // 16, 1.0, 0.0).astype(BF16)
    for i in range(NS):
        group = lg[pl.ds(NM * i, NM)].reshape(128, 256)
        lu[pl.ds(128 * i, 128)] = dot(perm, group).astype(BF16)

    ss[...] = jnp.zeros_like(ss)

    @pl.loop(0, NG)
    def _(j):
        cols = pl.ds(pl.multiple_of(j * 256, 256), 256)
        x0 = h_v[:, cols].astype(F32) + dot(lu[...], upg[j])
        sq = x0 * x0
        ss[...] += sq[:, :128] + sq[:, 128:]

    l_kv.wait()
    my_cols = pl.ds(pl.multiple_of(me * 256, 256), 256)
    row8 = lax.broadcasted_iota(jnp.int32, (32, 32), 0)
    col8 = lax.broadcasted_iota(jnp.int32, (32, 32), 1)
    new_ok = (row8 // 8 == col8 // 8) & (lax.rem(col8, 8) <= lax.rem(row8, 8))
    slot = lax.broadcasted_iota(jnp.int32, (8, 256), 1)

    def attention(c):
        rows = pl.ds(c * CROWS, CROWS)
        r = lax.rsqrt(jnp.sum(ss[rows], axis=-1, keepdims=True) * (1.0 / WIDTH) + 1e-05)
        lat = lu[rows]
        q, k, v = [(acc[t, rows] + dot(lat, mqb[t])) * r for t in range(3)]
        cosine, sine = cos_v[rows], sin_v[rows]

        def rope(z):
            return (z * cosine + pltpu.roll(z, 64, 1) * sine).astype(BF16)

        for hd in range(2):
            cut = slice(128 * hd, 128 * hd + 128)
            qh, kh, vh = rope(q[:, cut]), rope(k[:, cut]), v[:, cut].astype(BF16)
            pieces = []
            for i in range(CROWS // 32):
                d0 = c * (CROWS // 8) + 4 * i
                sub = slice(32 * i, 32 * i + 32)
                keys = kv_v[0, pl.ds(d0, 4), hd].reshape(256, 128)
                values = kv_v[1, pl.ds(d0, 4), hd].reshape(256, 128)
                old = dot_t(qh[sub], keys) * (1.0 / math.sqrt(128.0))
                parts = []
                for d in range(4):
                    ok = (slot >= 64 * d) & (slot < 64 * d + len_ref[d0 + d])
                    parts.append(jnp.where(ok, old[8 * d : 8 * d + 8], NEG))
                old = jnp.concatenate(parts, axis=0)
                new = dot_t(qh[sub], kh[sub]) * (1.0 / math.sqrt(128.0))
                new = jnp.where(new_ok, new, NEG)
                top = jnp.maximum(
                    jnp.max(old, axis=-1, keepdims=True), jnp.max(new, axis=-1, keepdims=True)
                )
                old = jnp.exp(old - top)
                new = jnp.exp(new - top)
                total = jnp.sum(old, axis=-1, keepdims=True) + jnp.sum(
                    new, axis=-1, keepdims=True
                )
                mixed = dot(old.astype(BF16), values) + dot(new.astype(BF16), vh[sub])
                pieces.append((mixed / total).astype(BF16))
            attn_g[s, rows, pl.ds(128 * hd, 128)] = jnp.concatenate(pieces, axis=0)

    at = {}

    def stage_a(c):
        attention(c)
        rows = pl.ds(c * CROWS, CROWS)
        piece = attn_g.at[s, rows]
        at["t1", c] = send(piece, piece, ds=c1)
        at["t2", c] = send(piece, piece, ds=y1)

    def stage_f(c):
        at["t2", c].wait_recv()
        piece = attn_g.at[y1, pl.ds(c * CROWS, CROWS)]
        at["t3", c] = send(piece, piece, ds=c1)

    def stage_o(c):
        if c == 0:
            l_wo.wait()
            for copy in wo_copies:
                copy.wait_recv()
        at["t1", c].wait_recv()
        at["t3", c].wait_recv()
        rows = pl.ds(c * CROWS, CROWS)
        for t in range(NM):
            cols = pl.ds(256 * t, 256)
            proj = dot(attn_g[0, rows], wo_v[0, :, cols])
            for i in range(1, NS):
                proj = proj + dot(attn_g[i, rows], wo_v[i, :, cols])
            psend[t, rows] = proj.astype(BF16)
        at["p", c] = [
            send(psend.at[t, rows], precv.at[m, rows], dm=t) for t in (xp, xm, xd)
        ]

    def lanes(dst_s, dst_m, half):
        start = (dst_s * NM + dst_m) * 256 + 128 * half
        return pl.ds(pl.multiple_of(start, 128), 128)

    def piece_of(c, owner_s, owner_m, half, lower=0, count=CROWS):
        return outv.at[pl.ds(c * CROWS + lower, count), lanes(owner_s, owner_m, half)]

    def move(name, c, piece, **to):
        at[name, c] = send(piece, piece, **to)

    def stage_r(c):
        for copy in at["p", c]:
            copy.wait_recv()
        rows = pl.ds(c * CROWS, CROWS)
        total = psend[m, rows].astype(F32)
        for t in (xp, xm, xd):
            total = total + precv[t, rows].astype(F32)
        x0 = h_v[rows, my_cols].astype(F32) + dot(lu[rows], upg[me])
        outv[rows, my_cols] = (x0 + total).astype(BF16)
        own_a = piece_of(c, s, m, 0)
        own_b = piece_of(c, s, m, 1)
        move("a1", c, own_a, ds=y1)
        move("b1", c, own_b, dm=xp)
        move("b2", c, own_b, dm=xm)
        move("a2", c, own_a, dm=xp)
        move("a3", c, own_a, dm=xm)
        move("b3", c, own_b, ds=y1)

    def stage_g(c):
        half = CROWS // 2
        at["a1", c].wait_recv()
        ypiece = piece_of(c, y1, m, 0)
        move("a4", c, ypiece, dm=xp)
        move("a5", c, ypiece, dm=xm)
        at["b1", c].wait_recv()
        move("b4", c, piece_of(c, s, xm, 1, 0, half), dm=xp)
        move("b6", c, piece_of(c, s, xm, 1), ds=y1)
        at["b2", c].wait_recv()
        move("b5", c, piece_of(c, s, xp, 1, half, half), dm=xm)
        move("b7", c, piece_of(c, s, xp, 1), ds=y1)
        at["a2", c].wait_recv()
        move("a6", c, piece_of(c, s, xm, 0), dm=xp)

    def stage_h(c):
        half = CROWS // 2
        at["a4", c].wait_recv()
        at["a5", c].wait_recv()
        move("a7", c, piece_of(c, y1, xp, 0), dm=xm)
        at["b4", c].wait_recv()
        move("b8", c, piece_of(c, s, xd, 1, 0, half), ds=y1)
        at["b5", c].wait_recv()
        move("b9", c, piece_of(c, s, xd, 1, half, half), ds=y1)

    def stage_i(c):
        for name in ("a3", "a6", "a7", "b3", "b6", "b7", "b8", "b9"):
            at[name, c].wait_recv()
        rows = pl.ds(c * CROWS, CROWS)
        for name, owner in (("f1", s), ("f2", y1)):
            piece = outv.at[rows, pl.ds(pl.multiple_of(owner * 1024, 1024), 1024)]
            move(name, c, piece, ds=c1)

    stores = []

    def stage_j(c):
        at["f1", c].wait_recv()
        at["f2", c].wait_recv()
        rows = pl.ds(c * CROWS, CROWS)
        stores.append(load(outv.at[rows], out_hbm.at[rows]))

    codec = {}

    def codec_send(layer):
        state = codec["state"]
        excited = jnp.where(state > 0, state, jnp.exp(jnp.minimum(state, 0.0)) - 1.0)
        place = el_v.at[layer, pl.ds(32, 128), pl.ds(pl.multiple_of(m * 128, 128), 128)]
        place[...] = excited.astype(BF16)
        codec["copies"] = [send(place, place, dm=t) for t in (xp, xm, xd)]

    def codec_start():
        for copy in lm_copies:
            copy.wait_recv()
        l_dp.wait()
        l_cw.wait()
        l_cs.wait()
        codec["state"] = dot(lmg[...].reshape(128, 256), dp_v[...])
        codec_send(0)

    def codec_step(layer):
        for copy in codec["copies"]:
            copy.wait_recv()
        state = codec["state"]
        for tap in range(3):
            state = state + dot(el_v[layer, pl.ds(16 * tap, 128), :], cw_v[layer, tap])
        codec["state"] = state
        if layer < 3:
            codec_send(layer + 1)
        else:
            decv[...] = dot(perm, state.astype(BF16)).astype(BF16)
            stores.append(load(decv, dec_hbm))

    stages = [stage_a, stage_f, stage_o, stage_r, stage_g, stage_h, stage_i, stage_j]
    for step in range(NCHUNK + len(stages) - 1):
        if step == 1:
            codec_start()
        if 3 <= step <= 6:
            codec_step(step - 3)
        for depth in reversed(range(len(stages))):
            c = step - depth
            if 0 <= c < NCHUNK:
                stages[depth](c)

    for copy in sends:
        copy.wait_send()
    for done in (tok_done, pu_done, pm_done, lg_done):
        done()
    for copy in stores:
        copy.wait()


N_LOCAL = 32
N_REMOTE = 192


def per_device(
    hidden_in,
    model_tokens,
    user_tokens,
    codebooks,
    decode_proj,
    conv_weight,
    conv_state,
    user_proj,
    norm_gain,
    w_qkv,
    w_out,
    kv_cache,
    cache_len,
):
    any_space = pl.BlockSpec(memory_space=pl.ANY)
    smem = pl.BlockSpec(memory_space=pltpu.SMEM)
    vmem = pltpu.VMEM
    out, dec = pl.pallas_call(
        kernel,
        out_shape=(
            jax.ShapeDtypeStruct((ROWS, WIDTH), BF16),
            jax.ShapeDtypeStruct((128, 128), BF16),
        ),
        in_specs=[any_space] * 12 + [smem],
        out_specs=(any_space, any_space),
        scratch_shapes=[
            vmem((ROWS, WIDTH), BF16),
            vmem((2, 8, 8, 16), jnp.int32),
            vmem((1024, 256), BF16),
            vmem((256, 128), BF16),
            vmem((4, 3, 512, 128), BF16),
            vmem((4, 160, 512), BF16),
            vmem((1, WIDTH), F32),
            vmem((3, WIDTH, 256), BF16),
            vmem((NS, 256, 1024), BF16),
            vmem((2, 64, 2, 64, 128), BF16),
            vmem((NG, 256, 256), BF16),
            vmem((8, 128), jnp.int32),
            vmem((NB, 8, 128), jnp.int32),
            vmem((512, 1024), BF16),
            vmem((512, 1024), BF16),
            vmem((NB, 32, 256), BF16),
            vmem((NB, 32, 256), BF16),
            vmem((NB, 32, 256), BF16),
            vmem((NB, 32, 256), BF16),
            vmem((NG, 32, 256), BF16),
            vmem((NM, 32, 256), BF16),
            vmem((ROWS, 256), BF16),
            vmem((3, 256, 256), F32),
            vmem((3, 256, 256), BF16),
            vmem((3, ROWS, 256), F32),
            vmem((ROWS, 128), F32),
            vmem((ROWS, 128), F32),
            vmem((ROWS, 128), F32),
            vmem((NS, ROWS, 256), BF16),
            vmem((NM, ROWS, 256), BF16),
            vmem((NM, ROWS, 256), BF16),
            vmem((ROWS, WIDTH), BF16),
            vmem((128, 128), BF16),
            pltpu.SemaphoreType.DMA((N_LOCAL,)),
            pltpu.SemaphoreType.DMA((N_REMOTE,)),
            pltpu.SemaphoreType.DMA((N_REMOTE,)),
        ],
        compiler_params=pltpu.CompilerParams(
            collective_id=0, has_side_effects=True, vmem_limit_bytes=56 * 1024 * 1024
        ),
        cost_estimate=pl.CostEstimate(
            flops=12_000_000_000, bytes_accessed=30_000_000, transcendentals=1_000_000
        ),
    )(
        hidden_in.reshape(ROWS, WIDTH),
        jnp.transpose(model_tokens, (1, 2, 0)),
        jnp.transpose(user_tokens, (1, 2, 0)),
        codebooks.reshape(1024, 256),
        decode_proj,
        conv_weight,
        jnp.transpose(conv_state, (1, 2, 0, 3)).reshape(4, 32, 512),
        user_proj,
        norm_gain.astype(F32).reshape(1, WIDTH),
        jnp.transpose(w_qkv, (1, 0, 2)),
        w_out,
        kv_cache,
        cache_len,
    )
    return out.reshape(64, 8, WIDTH), dec.reshape(16, 8, 128)


def solution(mesh):
    in_specs = (
        P("batch", None, None),
        P(("batch", "section"), None, None),
        P(("batch", "section"), None, None),
        P(None, "batch", None),
        P(None, "mp"),
        P(None, None, None, "mp"),
        P(("batch", "section"), None, None, None),
        P(None, ("section", "mp")),
        P(),
        P(None, None, ("section", "mp")),
        P(("section", "mp"), None),
        P(None, "batch", ("section", "mp"), None, None),
        P("batch"),
    )
    out_specs = (P("batch", None, None), P(("batch", "section"), None, "mp"))
    return jax.shard_map(
        per_device, mesh=mesh, in_specs=in_specs, out_specs=out_specs, check_vma=False
    )
```

```python
import functools
import math

import jax
import jax.numpy as jnp
from jax import lax
from jax.experimental import pallas as pl
from jax.experimental.pallas import tpu as pltpu
from jax.sharding import PartitionSpec as P

F32 = jnp.float32
BF16 = jnp.bfloat16
MESH = pl.DeviceIdType.MESH

NS, NB, NM = 4, 16, 4
NG = NS * NM
ROWS = 512
WIDTH = 4096
NCHUNK = 4
CROWS = ROWS // NCHUNK
NEG = -1e30


def dot(a, b):
    return jnp.dot(a, b, preferred_element_type=F32)


def dot_t(a, b):
    return lax.dot_general(a, b, (((1,), (1,)), ((), ())), preferred_element_type=F32)


class Sems:
    def __init__(self):
        self.used = 0

    def take(self, count=1):
        first = self.used
        self.used += count
        return first


def kernel(
    h_hbm,
    mt_hbm,
    ut_hbm,
    cb_hbm,
    dp_hbm,
    cw_hbm,
    cs_hbm,
    up_hbm,
    g_hbm,
    w_hbm,
    wo_hbm,
    kv_hbm,
    len_ref,
    outv,
    decv,
    h_v,
    tok_v,
    cb_v,
    dp_v,
    cw_v,
    cs_v,
    el_v,
    st_v,
    g32_v,
    g_v,
    w_v,
    wo_v,
    kv_v,
    upg,
    tsend,
    trecv,
    tt,
    oh,
    part,
    recv,
    lg,
    lmg,
    lu,
    mq,
    mqb,
    acc,
    ss,
    cos_v,
    sin_v,
    attn_g,
    psend,
    ra_y,
    a2,
    rap,
    ram,
    a3p,
    a3m,
    ra2p,
    ra2m,
    rbp,
    rbm,
    b2p,
    b2m,
    rb2p,
    rb2m,
    b_own,
    b_y,
    rby,
    lsem,
    ssem,
    rsem,
):
    s = lax.axis_index("section")
    b = lax.axis_index("batch")
    m = lax.axis_index("mp")
    me = s * NM + m
    core = lax.rem(s, 2)
    y = s // 2
    c1 = s + 1 - 2 * core
    y1 = lax.rem(s + 2, NS)
    xp = lax.rem(m + 1, NM)
    xm = lax.rem(m + NM - 1, NM)
    xd = lax.rem(m + 2, NM)

    local = Sems()
    remote = Sems()
    finish = []

    def load(src, dst):
        copy = pltpu.make_async_copy(src, dst, lsem.at[local.take()])
        copy.start()
        return copy

    def remote_copy(src, dst, at, ds=None, db=None, dm=None):
        return pltpu.make_async_remote_copy(
            src_ref=src,
            dst_ref=dst,
            send_sem=ssem.at[at],
            recv_sem=rsem.at[at],
            device_id=(
                s if ds is None else ds,
                b if db is None else db,
                m if dm is None else dm,
            ),
            device_id_type=MESH,
        )

    def send(src, dst, **to):
        copy = remote_copy(src, dst, remote.take(), **to)
        copy.start()
        finish.append(copy.wait_send)
        return copy

    class Spread:
        def __init__(self, axis, src, dst, count=1):
            self.base = remote.take(15 * count)
            self.axis, self.src, self.dst, self.count = axis, src, dst, count
            finish.append(self.wait_send)

        def make(self, k, which):
            at = self.base + 15 * which + k - 1
            if self.axis == "batch":
                target = lax.rem(b + k, NB)
                return remote_copy(self.src(target, which), self.dst(which), at, db=target)
            target = lax.rem(me + k, NG)
            return remote_copy(
                self.src(target, which),
                self.dst(which),
                at,
                ds=target // NM,
                dm=lax.rem(target, NM),
            )

        def start(self, which=0):
            @pl.loop(1, 16)
            def _(k):
                self.make(k, which).start()

        def wait_recv(self, which=0):
            @pl.loop(1, 16)
            def _(k):
                self.make(k, which).wait_recv()

        def wait_send(self):
            for which in range(self.count):

                @pl.loop(1, 16)
                def _(k):
                    self.make(k, which).wait_send()

    class Event:
        def __init__(self, src, dst, count=NCHUNK, **to):
            self.base = remote.take(count)
            self.src, self.dst, self.to, self.count = src, dst, to, count
            finish.append(self.wait_sends)

        def make(self, c):
            return remote_copy(self.src(c), self.dst(c), self.base + c, **self.to)

        def start(self, c):
            self.make(c).start()

        def wait(self, c):
            self.make(c).wait_recv()

        def wait_sends(self):
            @pl.loop(0, self.count)
            def _(c):
                self.make(c).wait_send()

    l_ut = load(ut_hbm, tok_v.at[0])
    l_mt = load(mt_hbm, tok_v.at[1])
    l_up = load(up_hbm, upg.at[me])
    l_cb = load(cb_hbm, cb_v)
    l_g = load(g_hbm, g32_v)
    l_h = load(h_hbm, h_v)
    l_w = load(w_hbm, w_v)
    l_wo = []
    for yy in range(2):
        cols = pl.ds(pl.multiple_of((2 * yy + core) * 1024, 1024), 1024)
        l_wo.append(load(wo_hbm.at[:, cols], wo_v.at[core, yy]))
    l_cs = load(cs_hbm, cs_v)
    l_kv = load(kv_hbm, kv_v)
    l_dp = load(dp_hbm, dp_v)
    l_cw = load(cw_hbm, cw_v)

    barrier = pltpu.get_barrier_semaphore()

    @pl.loop(1, 16)
    def _(k):
        pl.semaphore_signal(
            barrier, inc=1, device_id=(s, lax.rem(b + k, NB), m), device_id_type=MESH
        )
        other = lax.rem(me + k, NG)
        pl.semaphore_signal(
            barrier, inc=1, device_id=(other // NM, b, lax.rem(other, NM)), device_id_type=MESH
        )

    l_ut.wait()
    l_mt.wait()
    f0 = 2 * m
    tile = jnp.concatenate(
        [
            tok_v[0, f0],
            tok_v[0, f0 + 1],
            tok_v[1, f0],
            tok_v[1, f0 + 1],
            jnp.zeros((8, 64), jnp.int32),
        ],
        axis=1,
    )
    tsend[...] = tile
    trecv[b] = tile
    pl.semaphore_wait(barrier, 30)
    tok = Spread("batch", lambda t, w: tsend, lambda w: trecv.at[b])
    tok.start()

    def up_send(block, **to):
        return send(upg.at[block], upg.at[block], **to)

    l_up.wait()
    u_y = up_send(me, ds=y1)
    u_p = up_send(me, dm=xp)
    u_m = up_send(me, dm=xm)
    wo_copies = []
    for yy in range(2):
        cols = pl.ds(pl.multiple_of((2 * yy + 1 - core) * 1024, 1024), 1024)
        wo_copies.append(send(wo_hbm.at[:, cols], wo_v.at[core, yy], ds=c1))

    lane = lax.broadcasted_iota(jnp.int32, (64, 128), 1)
    freq = jnp.exp(lax.rem(lane, 64).astype(F32) * (-2.0 * math.log(10000.0) / 128.0))
    frame = lax.rem(lax.broadcasted_iota(jnp.int32, (64, 128), 0), 8)

    @pl.loop(0, 8)
    def _(i):
        where = lax.broadcasted_iota(jnp.int32, (64, 128), 0) // 8
        pos = frame
        for d in range(8):
            pos = pos + jnp.where(where == d, len_ref[i * 8 + d], 0)
        angle = pos.astype(F32) * freq
        rows = pl.ds(pl.multiple_of(i * 64, 64), 64)
        cos_v[rows] = jnp.cos(angle)
        sine = jnp.sin(angle)
        sin_v[rows] = jnp.where(lane < 64, -sine, sine)

    l_g.wait()
    gain = g32_v[...].astype(F32)
    for i in range(32):
        g_v[:, pl.ds(128 * i, 128)] = gain[i : i + 1]

    u_y.wait_recv()
    yblk = y1 * NM + m
    u_yp = up_send(yblk, dm=xp)
    u_ym = up_send(yblk, dm=xm)

    tok.wait_recv()
    l_cb.wait()

    @pl.loop(0, NB)
    def _(i):
        tt[i] = trecv[i].T[:64]

    entry = lax.broadcasted_iota(jnp.int32, (32, 128), 1) + 128 * b
    pieces = Spread("batch", lambda t, w: part.at[w, t], lambda w: recv.at[w, b], 2)

    @pl.loop(0, 2)
    def _(which):
        @pl.loop(0, NB)
        def _(i):
            rows = tt[i, pl.ds(pl.multiple_of(32 * which, 32), 32), :]
            for c in range(8):
                hot = jnp.where(rows[:, c : c + 1] == entry, 1.0, 0.0).astype(BF16)
                oh[pl.ds(pl.multiple_of(i * 32, 32), 32), pl.ds(c * 128, 128)] = hot

        @pl.loop(0, 4)
        def _(i):
            rows = pl.ds(pl.multiple_of(i * 128, 128), 128)
            piece = dot(oh[rows], cb_v[...]).astype(BF16).reshape(4, 32, 256)
            part[which, pl.ds(4 * i, 4)] = piece

        pieces.start(which)
        recv[which, b] = part[which, b]

    u_p.wait_recv()
    u_f = up_send(s * NM + xm, dm=xp)
    u_m.wait_recv()
    u_yp.wait_recv()
    u_ym.wait_recv()
    u_yf = up_send(y1 * NM + xp, dm=xm)

    l_h.wait()
    l_w.wait()
    acc[...] = jnp.zeros_like(acc)

    @pl.loop(0, 8)
    def _(step):
        cols = pl.ds(pl.multiple_of(step * 512, 512), 512)
        scaled = (h_v[:, cols].astype(F32) * g_v[:, cols]).astype(BF16)
        for j in range(3):
            acc[j] += dot(scaled, w_v[j, cols, :])

    def total_of(which):
        def step(i, total):
            return total + recv[which, i].astype(F32)

        return lax.fori_loop(0, NB, step, jnp.zeros((32, 256), F32)).astype(BF16)

    pieces.wait_recv(0)
    lg[me] = total_of(0)
    latents = Spread("group", lambda t, w: lg.at[me], lambda w: lg.at[me])
    latents.start()

    u_f.wait_recv()
    u_yf.wait_recv()
    mine = pl.ds(pl.multiple_of(s * NM, NM), NM)
    yours = pl.ds(pl.multiple_of(y1 * NM, NM), NM)
    u_c = [up_send(mine, ds=c1), up_send(yours, ds=c1)]

    pieces.wait_recv(1)
    lmg[m] = total_of(1)
    lm_copies = [send(lmg.at[m], lmg.at[m], dm=t) for t in (xp, xm, xd)]

    mq[...] = jnp.zeros_like(mq)
    for copy in u_c:
        copy.wait_recv()

    @pl.loop(0, NG)
    def _(j):
        cols = pl.ds(pl.multiple_of(j * 256, 256), 256)
        scaled = (upg[j].astype(F32) * g_v[:, cols]).astype(BF16)
        for t in range(3):
            mq[t] += dot(scaled, w_v[t, cols, :])

    mqb[...] = mq[...].astype(BF16)

    latents.wait_recv()
    to = lax.broadcasted_iota(jnp.int32, (128, 128), 0)
    frm = lax.broadcasted_iota(jnp.int32, (128, 128), 1)
    perm = jnp.where(frm == lax.rem(to, 8) * 16 + to // 8, 1.0, 0.0).astype(BF16)

    @pl.loop(0, NS)
    def _(i):
        group = lg[pl.ds(NM * i, NM)].reshape(128, 256)
        lu[pl.ds(pl.multiple_of(128 * i, 128), 128)] = dot(perm, group).astype(BF16)

    ss[...] = jnp.zeros_like(ss)

    @pl.loop(0, NG)
    def _(j):
        cols = pl.ds(pl.multiple_of(j * 256, 256), 256)
        x0 = h_v[:, cols].astype(F32) + dot(lu[...], upg[j])
        sq = x0 * x0
        ss[...] += sq[:, :128] + sq[:, 128:]

    l_kv.wait()
    for copy in l_wo:
        copy.wait()
    for copy in wo_copies:
        copy.wait_recv()
    l_dp.wait()
    l_cw.wait()
    l_cs.wait()

    my_cols = pl.ds(pl.multiple_of(me * 256, 256), 256)
    row8 = lax.broadcasted_iota(jnp.int32, (32, 32), 0)
    col8 = lax.broadcasted_iota(jnp.int32, (32, 32), 1)
    new_ok = (row8 // 8 == col8 // 8) & (lax.rem(col8, 8) <= lax.rem(row8, 8))
    slot = lax.broadcasted_iota(jnp.int32, (8, 256), 1)

    def span(c, lower=0, count=CROWS):
        start = pl.multiple_of(c * CROWS + lower, CROWS // 2)
        return pl.ds(start, count)

    half = CROWS // 2

    def lo(c):
        return span(c, 0, half)

    def hi(c):
        return span(c, half, half)

    def attention(c):
        rows = span(c)
        r = lax.rsqrt(jnp.sum(ss[rows], axis=-1, keepdims=True) * (1.0 / WIDTH) + 1e-05)
        lat = lu[rows]
        q, k, v = [(acc[t, rows] + dot(lat, mqb[t])) * r for t in range(3)]
        cosine, sine = cos_v[rows], sin_v[rows]

        def rope(z):
            return (z * cosine + pltpu.roll(z, 64, 1) * sine).astype(BF16)

        for hd in range(2):
            cut = slice(128 * hd, 128 * hd + 128)
            qh, kh, vh = rope(q[:, cut]), rope(k[:, cut]), v[:, cut].astype(BF16)
            pieces = []
            for i in range(CROWS // 32):
                d0 = c * (CROWS // 8) + 4 * i
                sub = slice(32 * i, 32 * i + 32)
                keys = kv_v[0, pl.ds(d0, 4), hd].reshape(256, 128)
                values = kv_v[1, pl.ds(d0, 4), hd].reshape(256, 128)
                old = dot_t(qh[sub], keys) * (1.0 / math.sqrt(128.0))
                parts = []
                for d in range(4):
                    ok = (slot >= 64 * d) & (slot < 64 * d + len_ref[d0 + d])
                    parts.append(jnp.where(ok, old[8 * d : 8 * d + 8], NEG))
                old = jnp.concatenate(parts, axis=0)
                new = dot_t(qh[sub], kh[sub]) * (1.0 / math.sqrt(128.0))
                new = jnp.where(new_ok, new, NEG)
                top = jnp.maximum(
                    jnp.max(old, axis=-1, keepdims=True), jnp.max(new, axis=-1, keepdims=True)
                )
                old = jnp.exp(old - top)
                new = jnp.exp(new - top)
                total = jnp.sum(old, axis=-1, keepdims=True) + jnp.sum(
                    new, axis=-1, keepdims=True
                )
                mixed = dot(old.astype(BF16), values) + dot(new.astype(BF16), vh[sub])
                pieces.append((mixed / total).astype(BF16))
            attn_g[core, rows, pl.ds(128 * hd, 128)] = jnp.concatenate(pieces, axis=0)

    e_t = Event(lambda c: attn_g.at[core, span(c)], lambda c: attn_g.at[core, span(c)], ds=c1)
    lane_a, lane_b = pl.ds(0, 128), pl.ds(128, 128)
    e_ay = Event(lambda c: psend.at[1 - y, :, span(c), lane_a], lambda c: ra_y.at[:, span(c)], ds=y1)
    e_bp = Event(lambda c: psend.at[:, xd, lo(c), lane_b], lambda c: rbp.at[:, lo(c)], dm=xp)
    e_bm = Event(lambda c: psend.at[:, xd, hi(c), lane_b], lambda c: rbm.at[:, hi(c)], dm=xm)
    e_ap = Event(lambda c: a2.at[xd, lo(c)], lambda c: rap.at[lo(c)], dm=xp)
    e_am = Event(lambda c: a2.at[xd, hi(c)], lambda c: ram.at[hi(c)], dm=xm)
    e_bp2 = Event(lambda c: b2p.at[:, span(c)], lambda c: rb2p.at[:, span(c)], dm=xp)
    e_bm2 = Event(lambda c: b2m.at[:, span(c)], lambda c: rb2m.at[:, span(c)], dm=xm)
    e_ap2 = Event(lambda c: a3p.at[span(c)], lambda c: ra2p.at[span(c)], dm=xp)
    e_am2 = Event(lambda c: a3m.at[span(c)], lambda c: ra2m.at[span(c)], dm=xm)
    e_by = Event(lambda c: b_y.at[span(c)], lambda c: rby.at[span(c)], ds=y1)

    def gather(owner_s, owner_m, lane_half, rows, **to):
        def at(c):
            start = (owner_s * NM + owner_m) * 256 + 128 * lane_half
            return outv.at[rows(c), pl.ds(pl.multiple_of(start, 128), 128)]

        return Event(at, at, **to)

    g_a1 = gather(s, m, 0, span, ds=y1)
    g_a2 = gather(s, m, 0, span, dm=xp)
    g_a3 = gather(s, m, 0, span, dm=xm)
    g_a4 = gather(y1, m, 0, span, dm=xp)
    g_a5 = gather(y1, m, 0, span, dm=xm)
    g_a6 = gather(s, xm, 0, span, dm=xp)
    g_a7 = gather(y1, xp, 0, span, dm=xm)
    g_b1 = gather(s, m, 1, span, dm=xp)
    g_b2 = gather(s, m, 1, span, dm=xm)
    g_b3 = gather(s, m, 1, span, ds=y1)
    g_b4 = gather(s, xm, 1, lo, dm=xp)
    g_b5 = gather(s, xp, 1, hi, dm=xm)
    g_b6 = gather(s, xm, 1, span, ds=y1)
    g_b7 = gather(s, xp, 1, span, ds=y1)
    g_b8 = gather(s, xd, 1, lo, ds=y1)
    g_b9 = gather(s, xd, 1, hi, ds=y1)

    def wide(owner):
        def at(c):
            return outv.at[span(c), pl.ds(pl.multiple_of(owner * 1024, 1024), 1024)]

        return Event(at, at, ds=c1)

    g_f1 = wide(s)
    g_f2 = wide(y1)

    def stage_a(c):
        attention(c)
        e_t.start(c)

    def stage_o(c):
        e_t.wait(c)
        rows = span(c)
        for yy in range(2):
            proj = dot(attn_g[0, rows], wo_v[0, yy]) + dot(attn_g[1, rows], wo_v[1, yy])
            for t in range(NM):
                psend[yy, t, rows] = proj[:, 256 * t : 256 * t + 256].astype(BF16)
        e_ay.start(c)
        e_bp.start(c)
        e_bm.start(c)

    def stage_p(c):
        rows = span(c)
        e_bp.wait(c)
        e_bm.wait(c)
        for yy in range(2):
            b2p[yy, lo(c)] = (
                psend[yy, xp, lo(c), lane_b].astype(F32) + rbp[yy, lo(c)].astype(F32)
            ).astype(BF16)
            b2p[yy, hi(c)] = psend[yy, xp, hi(c), lane_b]
            b2m[yy, hi(c)] = (
                psend[yy, xm, hi(c), lane_b].astype(F32) + rbm[yy, hi(c)].astype(F32)
            ).astype(BF16)
            b2m[yy, lo(c)] = psend[yy, xm, lo(c), lane_b]
        e_bp2.start(c)
        e_bm2.start(c)
        e_ay.wait(c)
        for t in range(NM):
            a2[t, rows] = (
                psend[y, t, rows, lane_a].astype(F32) + ra_y[t, rows].astype(F32)
            ).astype(BF16)
        e_ap.start(c)
        e_am.start(c)

    def stage_q(c):
        rows = span(c)
        e_ap.wait(c)
        e_am.wait(c)
        a3p[lo(c)] = (a2[xp, lo(c)].astype(F32) + rap[lo(c)].astype(F32)).astype(BF16)
        a3p[hi(c)] = a2[xp, hi(c)]
        a3m[hi(c)] = (a2[xm, hi(c)].astype(F32) + ram[hi(c)].astype(F32)).astype(BF16)
        a3m[lo(c)] = a2[xm, lo(c)]
        e_ap2.start(c)
        e_am2.start(c)
        e_bp2.wait(c)
        e_bm2.wait(c)
        for where, yy in ((b_own, y), (b_y, 1 - y)):
            where[rows] = (
                psend[yy, m, rows, lane_b].astype(F32)
                + rb2p[yy, rows].astype(F32)
                + rb2m[yy, rows].astype(F32)
            ).astype(BF16)
        e_by.start(c)

    def stage_r(c):
        rows = span(c)
        x0 = h_v[rows, my_cols].astype(F32) + dot(lu[rows], upg[me])
        e_ap2.wait(c)
        e_am2.wait(c)
        first = a2[m, rows].astype(F32) + ra2p[rows].astype(F32) + ra2m[rows].astype(F32)
        e_by.wait(c)
        second = b_own[rows].astype(F32) + rby[rows].astype(F32)
        total = jnp.concatenate([first, second], axis=1)
        outv[rows, my_cols] = (x0 + total).astype(BF16)
        for event in (g_a1, g_b1, g_b2, g_a2, g_a3, g_b3):
            event.start(c)

    def stage_g(c):
        g_a1.wait(c)
        g_a4.start(c)
        g_a5.start(c)
        g_b1.wait(c)
        g_b4.start(c)
        g_b6.start(c)
        g_b2.wait(c)
        g_b5.start(c)
        g_b7.start(c)
        g_a2.wait(c)
        g_a6.start(c)

    def stage_h(c):
        g_a5.wait(c)
        g_a7.start(c)
        g_b4.wait(c)
        g_b8.start(c)
        g_b5.wait(c)
        g_b9.start(c)

    def stage_i(c):
        for event in (g_a3, g_a4, g_a6, g_a7, g_b3, g_b6, g_b7, g_b8, g_b9):
            event.wait(c)
        g_f1.start(c)
        g_f2.start(c)

    def stage_j(c):
        g_f1.wait(c)
        g_f2.wait(c)

    def excite(layer, state):
        excited = jnp.where(state > 0, state, jnp.exp(jnp.minimum(state, 0.0)) - 1.0)
        place = el_v.at[layer, pl.ds(32, 128), pl.ds(pl.multiple_of(m * 128, 128), 128)]
        place[...] = excited.astype(BF16)
        st_v[...] = state

    def codec_at(layer):
        return el_v.at[layer, pl.ds(32, 128), pl.ds(pl.multiple_of(m * 128, 128), 128)]

    codec_moves = [Event(codec_at, codec_at, dm=t) for t in (xp, xm, xd)]

    def codec_start():
        for copy in lm_copies:
            copy.wait_recv()
        excite(0, dot(lmg[...].reshape(128, 256), dp_v[...]))
        for move in codec_moves:
            move.start(0)

        @pl.loop(0, 4)
        def _(layer):
            rows = [cs_v[d, layer].astype(F32) for d in range(16)]
            for j in range(2):
                el_v[layer, pl.ds(16 * j, 16), :] = jnp.concatenate(
                    [row[j : j + 1] for row in rows], axis=0
                ).astype(BF16)

    def codec_step(layer):
        for move in codec_moves:
            move.wait(layer)
        state = st_v[...]
        for tap in range(3):
            state = state + dot(el_v[layer, pl.ds(16 * tap, 128), :], cw_v[layer, tap])
        st_v[...] = state

        @pl.when(layer < 3)
        def _():
            excite(layer + 1, state)
            for move in codec_moves:
                move.start(layer + 1)

    stages = [stage_j, stage_i, stage_h, stage_g, stage_r, stage_q, stage_p, stage_o]

    codec_start()

    @pl.loop(0, NCHUNK + len(stages))
    def _(step):
        pl.when(step < NCHUNK)(lambda: stage_a(step))
        for place, stage in enumerate(stages):
            c = step - (len(stages) - place)

            @pl.when((c >= 0) & (c < NCHUNK))
            def _():
                stage(c)

        @pl.when((step >= 1) & (step < 5))
        def _():
            codec_step(step - 1)

    decv[...] = dot(perm, st_v[...].astype(BF16)).astype(BF16)
    for done in finish:
        done()


N_LOCAL = 16
N_REMOTE = 256


def per_device(
    hidden_in,
    model_tokens,
    user_tokens,
    codebooks,
    decode_proj,
    conv_weight,
    conv_state,
    user_proj,
    norm_gain,
    w_qkv,
    w_out,
    kv_cache,
    cache_len,
):
    any_space = pl.BlockSpec(memory_space=pl.ANY)
    smem = pl.BlockSpec(memory_space=pltpu.SMEM)
    vmem = pltpu.VMEM
    out, dec = pl.pallas_call(
        kernel,
        out_shape=(vmem((ROWS, WIDTH), BF16), vmem((128, 128), BF16)),
        in_specs=[any_space] * 12 + [smem],
        out_specs=(pl.BlockSpec(memory_space=vmem), pl.BlockSpec(memory_space=vmem)),
        scratch_shapes=[
            vmem((ROWS, WIDTH), BF16),
            vmem((2, 8, 8, 16), jnp.int32),
            vmem((1024, 256), BF16),
            vmem((256, 128), BF16),
            vmem((4, 3, 512, 128), BF16),
            vmem((16, 4, 2, 512), BF16),
            vmem((4, 160, 512), BF16),
            vmem((128, 128), F32),
            vmem((32, 128), BF16),
            vmem((1, WIDTH), F32),
            vmem((3, WIDTH, 256), BF16),
            vmem((2, 2, 256, 1024), BF16),
            vmem((2, 64, 2, 64, 128), BF16),
            vmem((NG, 256, 256), BF16),
            vmem((8, 128), jnp.int32),
            vmem((NB, 8, 128), jnp.int32),
            vmem((NB, 64, 8), jnp.int32),
            vmem((512, 1024), BF16),
            vmem((2, NB, 32, 256), BF16),
            vmem((2, NB, 32, 256), BF16),
            vmem((NG, 32, 256), BF16),
            vmem((NM, 32, 256), BF16),
            vmem((ROWS, 256), BF16),
            vmem((3, 256, 256), F32),
            vmem((3, 256, 256), BF16),
            vmem((3, ROWS, 256), F32),
            vmem((ROWS, 128), F32),
            vmem((ROWS, 128), F32),
            vmem((ROWS, 128), F32),
            vmem((2, ROWS, 256), BF16),
            vmem((2, NM, ROWS, 256), BF16),
            vmem((NM, ROWS, 128), BF16),
            vmem((NM, ROWS, 128), BF16),
            vmem((ROWS, 128), BF16),
            vmem((ROWS, 128), BF16),
            vmem((ROWS, 128), BF16),
            vmem((ROWS, 128), BF16),
            vmem((ROWS, 128), BF16),
            vmem((ROWS, 128), BF16),
            vmem((2, ROWS, 128), BF16),
            vmem((2, ROWS, 128), BF16),
            vmem((2, ROWS, 128), BF16),
            vmem((2, ROWS, 128), BF16),
            vmem((2, ROWS, 128), BF16),
            vmem((2, ROWS, 128), BF16),
            vmem((ROWS, 128), BF16),
            vmem((ROWS, 128), BF16),
            vmem((ROWS, 128), BF16),
            pltpu.SemaphoreType.DMA((N_LOCAL,)),
            pltpu.SemaphoreType.DMA((N_REMOTE,)),
            pltpu.SemaphoreType.DMA((N_REMOTE,)),
        ],
        compiler_params=pltpu.CompilerParams(
            collective_id=0, has_side_effects=True, vmem_limit_bytes=59 * 1024 * 1024
        ),
        cost_estimate=pl.CostEstimate(
            flops=12_000_000_000, bytes_accessed=30_000_000, transcendentals=1_000_000
        ),
    )(
        hidden_in.reshape(ROWS, WIDTH),
        jnp.transpose(model_tokens, (1, 2, 0)),
        jnp.transpose(user_tokens, (1, 2, 0)),
        codebooks.reshape(1024, 256),
        decode_proj,
        conv_weight,
        conv_state,
        user_proj,
        norm_gain.reshape(32, 128),
        jnp.transpose(w_qkv, (1, 0, 2)),
        w_out,
        kv_cache,
        cache_len,
    )
    return out.reshape(64, 8, WIDTH), dec.reshape(16, 8, 128)


def solution(mesh):
    in_specs = (
        P("batch", None, None),
        P(("batch", "section"), None, None),
        P(("batch", "section"), None, None),
        P(None, "batch", None),
        P(None, "mp"),
        P(None, None, None, "mp"),
        P(("batch", "section"), None, None, None),
        P(None, ("section", "mp")),
        P(),
        P(None, None, ("section", "mp")),
        P(("section", "mp"), None),
        P(None, "batch", ("section", "mp"), None, None),
        P("batch"),
    )
    out_specs = (P("batch", None, None), P(("batch", "section"), None, "mp"))
    return jax.shard_map(
        per_device, mesh=mesh, in_specs=in_specs, out_specs=out_specs, check_vma=False
    )
```

```python
import functools
import math

import jax
import jax.numpy as jnp
from jax import lax
from jax.experimental import pallas as pl
from jax.experimental.pallas import tpu as pltpu
from jax.sharding import PartitionSpec as P

F32 = jnp.float32
BF16 = jnp.bfloat16
MESH = pl.DeviceIdType.MESH

NS, NB, NM = 4, 16, 4
NG = NS * NM
ROWS = 512
WIDTH = 4096
NCHUNK = 4
CROWS = ROWS // NCHUNK
NEG = -1e30


def dot(a, b):
    return jnp.dot(a, b, preferred_element_type=F32)


def dot_t(a, b):
    return lax.dot_general(a, b, (((1,), (1,)), ((), ())), preferred_element_type=F32)


class Sems:
    def __init__(self):
        self.used = 0

    def take(self, count=1):
        first = self.used
        self.used += count
        return first


def kernel(
    h_hbm,
    mt_hbm,
    ut_hbm,
    cb_hbm,
    dp_hbm,
    cw_hbm,
    cs_hbm,
    up_hbm,
    g_hbm,
    w_hbm,
    wo_hbm,
    kv_hbm,
    len_ref,
    outv,
    decv,
    h_v,
    tok_v,
    cb_v,
    dp_v,
    cw_v,
    cs_v,
    el_v,
    st_v,
    g32_v,
    g_v,
    w_v,
    wo_v,
    kv_v,
    upg,
    tsend,
    trecv,
    tt,
    part,
    recv,
    lg,
    lmg,
    lu,
    mq,
    mqb,
    acc,
    ss,
    cos_v,
    sin_v,
    attn_g,
    psend,
    ra_y,
    a2,
    rap,
    ram,
    ra2p,
    ra2m,
    rbp,
    rbm,
    rb2p,
    rb2m,
    b_own,
    b_y,
    rby,
    lsem,
    ssem,
    rsem,
):
    s = lax.axis_index("section")
    b = lax.axis_index("batch")
    m = lax.axis_index("mp")
    me = s * NM + m
    core = lax.rem(s, 2)
    y = s // 2
    c1 = s + 1 - 2 * core
    y1 = lax.rem(s + 2, NS)
    xp = lax.rem(m + 1, NM)
    xm = lax.rem(m + NM - 1, NM)
    xd = lax.rem(m + 2, NM)

    local = Sems()
    remote = Sems()
    finish = []

    def load(src, dst):
        copy = pltpu.make_async_copy(src, dst, lsem.at[local.take()])
        copy.start()
        return copy

    def remote_copy(src, dst, at, ds=None, db=None, dm=None):
        return pltpu.make_async_remote_copy(
            src_ref=src,
            dst_ref=dst,
            send_sem=ssem.at[at],
            recv_sem=rsem.at[at],
            device_id=(
                s if ds is None else ds,
                b if db is None else db,
                m if dm is None else dm,
            ),
            device_id_type=MESH,
        )

    def send(src, dst, **to):
        copy = remote_copy(src, dst, remote.take(), **to)
        copy.start()
        finish.append(copy.wait_send)
        return copy

    class Spread:
        def __init__(self, axis, src, dst, count=1):
            self.base = remote.take(15 * count)
            self.axis, self.src, self.dst, self.count = axis, src, dst, count
            finish.append(self.wait_send)

        def make(self, k, which):
            at = self.base + 15 * which + k - 1
            if self.axis == "batch":
                target = lax.rem(b + k, NB)
                return remote_copy(self.src(k, which), self.dst(which), at, db=target)
            target = lax.rem(me + k, NG)
            return remote_copy(
                self.src(k, which),
                self.dst(which),
                at,
                ds=target // NM,
                dm=lax.rem(target, NM),
            )

        def start(self, which=0):
            @pl.loop(1, 16)
            def _(k):
                self.make(k, which).start()

        def wait_recv(self, which=0):
            @pl.loop(1, 16)
            def _(k):
                self.make(k, which).wait_recv()

        def wait_send(self):
            for which in range(self.count):

                @pl.loop(1, 16)
                def _(k):
                    self.make(k, which).wait_send()

    class Event:
        def __init__(self, src, dst, count=NCHUNK, **to):
            self.base = remote.take(count)
            self.src, self.dst, self.to, self.count = src, dst, to, count
            finish.append(self.wait_sends)

        def make(self, c):
            return remote_copy(self.src(c), self.dst(c), self.base + c, **self.to)

        def start(self, c):
            self.make(c).start()

        def wait(self, c):
            self.make(c).wait_recv()

        def wait_sends(self):
            @pl.loop(0, self.count)
            def _(c):
                self.make(c).wait_send()

    barrier = pltpu.get_barrier_semaphore()

    @pl.loop(1, 16)
    def _(k):
        pl.semaphore_signal(
            barrier, inc=1, device_id=(s, lax.rem(b + k, NB), m), device_id_type=MESH
        )
        other = lax.rem(me + k, NG)
        pl.semaphore_signal(
            barrier, inc=1, device_id=(other // NM, b, lax.rem(other, NM)), device_id_type=MESH
        )

    l_ut = load(ut_hbm, tok_v.at[0])
    l_mt = load(mt_hbm, tok_v.at[1])
    l_up = load(up_hbm, upg.at[me])
    l_cb = load(cb_hbm, cb_v)
    l_g = load(g_hbm, g32_v)
    l_h = load(h_hbm, h_v)
    l_w = load(w_hbm, w_v)
    l_wo = []
    for yy in range(2):
        cols = pl.ds(pl.multiple_of((2 * yy + core) * 1024, 1024), 1024)
        l_wo.append(load(wo_hbm.at[:, cols], wo_v.at[core, yy]))
    l_cs = load(cs_hbm, cs_v)
    l_kv = load(kv_hbm, kv_v)
    l_dp = load(dp_hbm, dp_v)
    l_cw = load(cw_hbm, cw_v)

    l_ut.wait()
    l_mt.wait()
    f0 = 2 * m
    tile = jnp.concatenate(
        [
            tok_v[0, f0],
            tok_v[0, f0 + 1],
            tok_v[1, f0],
            tok_v[1, f0 + 1],
            jnp.zeros((8, 64), jnp.int32),
        ],
        axis=1,
    )
    tsend[...] = tile
    trecv[b] = tile
    pl.semaphore_wait(barrier, 30)
    tok = Spread("batch", lambda k, w: tsend, lambda w: trecv.at[b])
    tok.start()

    def up_send(block, **to):
        return send(upg.at[block], upg.at[block], **to)

    l_up.wait()
    u_y = up_send(me, ds=y1)
    u_p = up_send(me, dm=xp)
    u_m = up_send(me, dm=xm)
    wo_copies = []
    for yy in range(2):
        cols = pl.ds(pl.multiple_of((2 * yy + 1 - core) * 1024, 1024), 1024)
        wo_copies.append(send(wo_hbm.at[:, cols], wo_v.at[core, yy], ds=c1))

    lane = lax.broadcasted_iota(jnp.int32, (64, 128), 1)
    freq = jnp.exp(lax.rem(lane, 64).astype(F32) * (-2.0 * math.log(10000.0) / 128.0))
    frame = lax.rem(lax.broadcasted_iota(jnp.int32, (64, 128), 0), 8)

    @pl.loop(0, 8)
    def _(i):
        where = lax.broadcasted_iota(jnp.int32, (64, 128), 0) // 8
        pos = frame
        for d in range(8):
            pos = pos + jnp.where(where == d, len_ref[i * 8 + d], 0)
        angle = pos.astype(F32) * freq
        rows = pl.ds(pl.multiple_of(i * 64, 64), 64)
        cos_v[rows] = jnp.cos(angle)
        sine = jnp.sin(angle)
        sin_v[rows] = jnp.where(lane < 64, -sine, sine)

    l_g.wait()
    gain = g32_v[...].astype(F32)
    for i in range(32):
        g_v[:, pl.ds(128 * i, 128)] = gain[i : i + 1]

    u_y.wait_recv()
    yblk = y1 * NM + m
    u_yp = up_send(yblk, dm=xp)
    u_ym = up_send(yblk, dm=xm)

    tok.wait_recv()
    l_cb.wait()

    @pl.loop(0, NB)
    def _(k):
        tt[k] = trecv[lax.rem(b + k, NB)].T[:64]

    entry = lax.broadcasted_iota(jnp.int32, (128, 128), 1) + 128 * b
    pieces = Spread("batch", lambda k, w: part.at[w, k], lambda w: recv.at[w, b], 2)

    def look_up(which):
        @pl.loop(0, 4)
        def _(quad):
            rows = tt[pl.ds(4 * quad, 4), pl.ds(32 * which, 32), :].reshape(128, 8)
            hot = [jnp.where(rows[:, c : c + 1] == entry, 1.0, 0.0).astype(BF16) for c in range(8)]
            piece = dot(jnp.concatenate(hot, axis=1), cb_v[...])
            part[which, pl.ds(4 * quad, 4)] = piece.astype(BF16).reshape(4, 32, 256)

            if which == 0:

                @pl.loop(0, 4)
                def _(j):
                    k = 4 * quad + j

                    @pl.when(k > 0)
                    def _():
                        pieces.make(k, which).start()

        recv[which, b] = part[which, 0]

    look_up(0)

    u_p.wait_recv()
    u_f = up_send(s * NM + xm, dm=xp)
    u_m.wait_recv()
    u_yp.wait_recv()
    u_ym.wait_recv()
    u_yf = up_send(y1 * NM + xp, dm=xm)

    l_cs.wait()

    @pl.loop(0, 4)
    def _(layer):
        rows = [cs_v[d, layer].astype(F32) for d in range(16)]
        for j in range(2):
            el_v[layer, pl.ds(16 * j, 16), :] = jnp.concatenate(
                [row[j : j + 1] for row in rows], axis=0
            ).astype(BF16)

    l_h.wait()
    l_w.wait()
    acc[...] = jnp.zeros_like(acc)

    @pl.loop(0, 4)
    def _(step):
        cols = pl.ds(pl.multiple_of(step * 1024, 1024), 1024)
        scaled = (h_v[:, cols].astype(F32) * g_v[:, cols]).astype(BF16)
        for j in range(3):
            acc[j] += dot(scaled, w_v[j, cols, :])

    look_up(1)

    u_f.wait_recv()
    u_yf.wait_recv()
    mine = pl.ds(pl.multiple_of(s * NM, NM), NM)
    yours = pl.ds(pl.multiple_of(y1 * NM, NM), NM)
    u_c = [up_send(mine, ds=c1), up_send(yours, ds=c1)]

    def total_of(which):
        def step(i, total):
            return total + recv[which, i].astype(F32)

        return lax.fori_loop(0, NB, step, jnp.zeros((32, 256), F32)).astype(BF16)

    pieces.wait_recv(0)
    lg[me] = total_of(0)
    latents = Spread("group", lambda k, w: lg.at[me], lambda w: lg.at[me])
    latents.start()
    pieces.start(1)

    mq[...] = jnp.zeros_like(mq)
    for copy in u_c:
        copy.wait_recv()

    @pl.loop(0, NS)
    def _(j):
        cols = pl.ds(pl.multiple_of(j * 1024, 1024), 1024)
        wide_up = jnp.concatenate([upg[NM * j + i] for i in range(NM)], axis=1)
        scaled = (wide_up.astype(F32) * g_v[:, cols]).astype(BF16)
        for t in range(3):
            mq[t] += dot(scaled, w_v[t, cols, :])

    mqb[...] = mq[...].astype(BF16)

    latents.wait_recv()
    to = lax.broadcasted_iota(jnp.int32, (128, 128), 0)
    frm = lax.broadcasted_iota(jnp.int32, (128, 128), 1)
    perm = jnp.where(frm == lax.rem(to, 8) * 16 + to // 8, 1.0, 0.0).astype(BF16)

    @pl.loop(0, NS)
    def _(i):
        group = lg[pl.ds(NM * i, NM)].reshape(128, 256)
        lu[pl.ds(pl.multiple_of(128 * i, 128), 128)] = dot(perm, group).astype(BF16)

    ss[...] = jnp.zeros_like(ss)

    @pl.loop(0, NG, unroll=2)
    def _(j):
        cols = pl.ds(pl.multiple_of(j * 256, 256), 256)
        x0 = h_v[:, cols].astype(F32) + dot(lu[...], upg[j])
        sq = x0 * x0
        ss[...] += sq[:, :128] + sq[:, 128:]

    l_kv.wait()
    for copy in l_wo:
        copy.wait()
    for copy in wo_copies:
        copy.wait_recv()
    l_dp.wait()
    l_cw.wait()

    my_cols = pl.ds(pl.multiple_of(me * 256, 256), 256)
    row8 = lax.broadcasted_iota(jnp.int32, (32, 32), 0)
    col8 = lax.broadcasted_iota(jnp.int32, (32, 32), 1)
    new_ok = (row8 // 8 == col8 // 8) & (lax.rem(col8, 8) <= lax.rem(row8, 8))
    slot = lax.broadcasted_iota(jnp.int32, (8, 256), 1)

    def span(c, lower=0, count=CROWS):
        start = pl.multiple_of(c * CROWS + lower, CROWS // 2)
        return pl.ds(start, count)

    half = CROWS // 2

    def lo(c):
        return span(c, 0, half)

    def hi(c):
        return span(c, half, half)

    def attention(c):
        rows = span(c)
        r = lax.rsqrt(jnp.sum(ss[rows], axis=-1, keepdims=True) * (1.0 / WIDTH) + 1e-05)
        lat = lu[rows]
        q, k, v = [(acc[t, rows] + dot(lat, mqb[t])) * r for t in range(3)]
        cosine, sine = cos_v[rows], sin_v[rows]

        def rope(z):
            return (z * cosine + pltpu.roll(z, 64, 1) * sine).astype(BF16)

        for hd in range(2):
            cut = slice(128 * hd, 128 * hd + 128)
            qh, kh, vh = rope(q[:, cut]), rope(k[:, cut]), v[:, cut].astype(BF16)
            pieces = []
            for i in range(CROWS // 32):
                d0 = c * (CROWS // 8) + 4 * i
                sub = slice(32 * i, 32 * i + 32)
                keys = kv_v[0, pl.ds(d0, 4), hd].reshape(256, 128)
                values = kv_v[1, pl.ds(d0, 4), hd].reshape(256, 128)
                old = dot_t(qh[sub], keys) * (1.0 / math.sqrt(128.0))
                parts = []
                for d in range(4):
                    ok = (slot >= 64 * d) & (slot < 64 * d + len_ref[d0 + d])
                    parts.append(jnp.where(ok, old[8 * d : 8 * d + 8], NEG))
                old = jnp.concatenate(parts, axis=0)
                new = dot_t(qh[sub], kh[sub]) * (1.0 / math.sqrt(128.0))
                new = jnp.where(new_ok, new, NEG)
                top = jnp.maximum(
                    jnp.max(old, axis=-1, keepdims=True), jnp.max(new, axis=-1, keepdims=True)
                )
                old = jnp.exp(old - top)
                new = jnp.exp(new - top)
                total = jnp.sum(old, axis=-1, keepdims=True) + jnp.sum(
                    new, axis=-1, keepdims=True
                )
                mixed = dot(old.astype(BF16), values) + dot(new.astype(BF16), vh[sub])
                pieces.append((mixed / total).astype(BF16))
            attn_g[core, rows, pl.ds(128 * hd, 128)] = jnp.concatenate(pieces, axis=0)

    e_t = Event(lambda c: attn_g.at[core, span(c)], lambda c: attn_g.at[core, span(c)], ds=c1)
    lane_a, lane_b = pl.ds(0, 128), pl.ds(128, 128)
    e_ay = Event(lambda c: psend.at[1 - y, :, span(c), lane_a], lambda c: ra_y.at[:, span(c)], ds=y1)
    e_bp = Event(lambda c: psend.at[:, xd, lo(c), lane_b], lambda c: rbp.at[:, lo(c)], dm=xp)
    e_bm = Event(lambda c: psend.at[:, xd, hi(c), lane_b], lambda c: rbm.at[:, hi(c)], dm=xm)
    e_ap = Event(lambda c: a2.at[xd, lo(c)], lambda c: rap.at[lo(c)], dm=xp)
    e_am = Event(lambda c: a2.at[xd, hi(c)], lambda c: ram.at[hi(c)], dm=xm)
    e_bp2 = Event(lambda c: psend.at[:, xp, span(c), lane_b], lambda c: rb2p.at[:, span(c)], dm=xp)
    e_bm2 = Event(lambda c: psend.at[:, xm, span(c), lane_b], lambda c: rb2m.at[:, span(c)], dm=xm)
    e_ap2 = Event(lambda c: a2.at[xp, span(c)], lambda c: ra2p.at[span(c)], dm=xp)
    e_am2 = Event(lambda c: a2.at[xm, span(c)], lambda c: ra2m.at[span(c)], dm=xm)
    e_by = Event(lambda c: b_y.at[span(c)], lambda c: rby.at[span(c)], ds=y1)

    def gather(owner, first, count, **to):
        def at(c):
            start = pl.multiple_of(owner * 256 + first, 128)
            return outv.at[span(c), pl.ds(start, count)]

        return Event(at, at, **to)

    g_p = gather(me, 0, 256, dm=xp)
    g_m = gather(me, 0, 256, dm=xm)
    g_y = gather(me, 0, 256, ds=y1)
    g_ap = gather(y1 * NM + m, 0, 128, dm=xp)
    g_am = gather(y1 * NM + m, 0, 128, dm=xm)
    g_pp = gather(s * NM + xm, 0, 128, dm=xp)
    g_mm = gather(s * NM + xp, 128, 128, dm=xm)
    g_bm = gather(s * NM + xm, 128, 128, ds=y1)
    g_bp = gather(s * NM + xp, 128, 128, ds=y1)
    g_ad = gather(y1 * NM + xm, 0, 128, dm=xp)
    g_bd = gather(s * NM + xd, 128, 128, ds=y1)
    g_f1 = gather(s * NM, 0, 1024, ds=c1)
    g_f2 = gather(y1 * NM, 0, 1024, ds=c1)

    def stage_a(c):
        attention(c)
        e_t.start(c)

    def stage_o(c):
        e_t.wait(c)
        rows = span(c)
        for yy in range(2):
            proj = dot(attn_g[0, rows], wo_v[0, yy]) + dot(attn_g[1, rows], wo_v[1, yy])
            for t in range(NM):
                psend[yy, t, rows] = proj[:, 256 * t : 256 * t + 256].astype(BF16)
        e_ay.start(c)
        e_bp.start(c)
        e_bm.start(c)

    def add(place, other):
        place[...] = (place[...].astype(F32) + other.astype(F32)).astype(BF16)

    def stage_p(c):
        rows = span(c)
        e_bp.wait(c)
        add(psend.at[:, xp, lo(c), lane_b], rbp[:, lo(c)])
        e_bp2.start(c)
        e_bm.wait(c)
        add(psend.at[:, xm, hi(c), lane_b], rbm[:, hi(c)])
        e_bm2.start(c)
        e_ay.wait(c)
        a2[:, rows] = (
            psend[y, :, rows, lane_a].astype(F32) + ra_y[:, rows].astype(F32)
        ).astype(BF16)
        e_ap.start(c)
        e_am.start(c)

    def stage_q(c):
        rows = span(c)
        e_ap.wait(c)
        add(a2.at[xp, lo(c)], rap[lo(c)])
        e_ap2.start(c)
        e_am.wait(c)
        add(a2.at[xm, hi(c)], ram[hi(c)])
        e_am2.start(c)
        e_bp2.wait(c)
        e_bm2.wait(c)

        def total(yy):
            ours = psend[yy, m, rows, lane_b].astype(F32)
            return ours + rb2p[yy, rows].astype(F32) + rb2m[yy, rows].astype(F32)

        b_y[rows] = total(1 - y).astype(BF16)
        e_by.start(c)
        b_own[rows] = total(y)

    def stage_r(c):
        rows = span(c)
        x0 = h_v[rows, my_cols].astype(F32) + dot(lu[rows], upg[me])
        e_ap2.wait(c)
        e_am2.wait(c)
        first = a2[m, rows].astype(F32) + ra2p[rows].astype(F32) + ra2m[rows].astype(F32)
        e_by.wait(c)
        second = b_own[rows] + rby[rows].astype(F32)
        total = jnp.concatenate([first, second], axis=1)
        outv[rows, my_cols] = (x0 + total).astype(BF16)
        for event in (g_y, g_p, g_m):
            event.start(c)

    def stage_g(c):
        g_y.wait(c)
        g_ap.start(c)
        g_am.start(c)
        g_p.wait(c)
        g_pp.start(c)
        g_bm.start(c)
        g_m.wait(c)
        g_mm.start(c)
        g_bp.start(c)

    def stage_h(c):
        g_ap.wait(c)
        g_ad.start(c)
        g_mm.wait(c)
        g_bd.start(c)
        g_pp.wait(c)
        g_f1.start(c)

    def stage_i(c):
        for event in (g_am, g_bm, g_bp, g_ad, g_bd):
            event.wait(c)
        g_f2.start(c)

    def stage_j(c):
        g_f1.wait(c)
        g_f2.wait(c)

    def excite(layer, state):
        excited = jnp.where(state > 0, state, jnp.exp(jnp.minimum(state, 0.0)) - 1.0)
        place = el_v.at[layer, pl.ds(32, 128), pl.ds(pl.multiple_of(m * 128, 128), 128)]
        place[...] = excited.astype(BF16)
        st_v[...] = state

    def codec_at(layer):
        return el_v.at[layer, pl.ds(32, 128), pl.ds(pl.multiple_of(m * 128, 128), 128)]

    codec_moves = [Event(codec_at, codec_at, 4, dm=t) for t in (xp, xm, xd)]

    lm_moves = [Event(lambda c: lmg.at[m], lambda c: lmg.at[m], 1, dm=t) for t in (xp, xm, xd)]

    def codec_latents():
        pieces.wait_recv(1)
        lmg[m] = total_of(1)
        for move in lm_moves:
            move.start(0)

    def codec_start():
        for move in lm_moves:
            move.wait(0)
        excite(0, dot(lmg[...].reshape(128, 256), dp_v[...]))
        for move in codec_moves:
            move.start(0)

    def codec_step(layer):
        for move in codec_moves:
            move.wait(layer)
        state = st_v[...]
        for tap in range(3):
            state = state + dot(el_v[layer, pl.ds(16 * tap, 128), :], cw_v[layer, tap])
        st_v[...] = state

        @pl.when(layer < 3)
        def _():
            excite(layer + 1, state)
            for move in codec_moves:
                move.start(layer + 1)

    stages = [stage_j, stage_i, stage_h, stage_g, stage_r, stage_q, stage_p, stage_o]

    @pl.loop(0, NCHUNK + len(stages))
    def _(step):
        pl.when(step < NCHUNK)(lambda: stage_a(step))
        for place, stage in enumerate(stages):
            c = step - (len(stages) - place)

            @pl.when((c >= 0) & (c < NCHUNK))
            def _():
                stage(c)

        pl.when(step == 2)(codec_latents)
        pl.when(step == 3)(codec_start)

        @pl.when((step >= 4) & (step < 8))
        def _():
            codec_step(step - 4)

    decv[...] = dot(perm, st_v[...].astype(BF16)).astype(BF16)
    for done in finish:
        done()


N_LOCAL = 16
N_REMOTE = 256


def per_device(
    hidden_in,
    model_tokens,
    user_tokens,
    codebooks,
    decode_proj,
    conv_weight,
    conv_state,
    user_proj,
    norm_gain,
    w_qkv,
    w_out,
    kv_cache,
    cache_len,
):
    any_space = pl.BlockSpec(memory_space=pl.ANY)
    smem = pl.BlockSpec(memory_space=pltpu.SMEM)
    vmem = pltpu.VMEM
    out, dec = pl.pallas_call(
        kernel,
        out_shape=(vmem((ROWS, WIDTH), BF16), vmem((128, 128), BF16)),
        in_specs=[any_space] * 12 + [smem],
        out_specs=(pl.BlockSpec(memory_space=vmem), pl.BlockSpec(memory_space=vmem)),
        scratch_shapes=[
            vmem((ROWS, WIDTH), BF16),
            vmem((2, 8, 8, 16), jnp.int32),
            vmem((1024, 256), BF16),
            vmem((256, 128), BF16),
            vmem((4, 3, 512, 128), BF16),
            vmem((16, 4, 2, 512), BF16),
            vmem((4, 160, 512), BF16),
            vmem((128, 128), F32),
            vmem((32, 128), BF16),
            vmem((1, WIDTH), F32),
            vmem((3, WIDTH, 256), BF16),
            vmem((2, 2, 256, 1024), BF16),
            vmem((2, 64, 2, 64, 128), BF16),
            vmem((NG, 256, 256), BF16),
            vmem((8, 128), jnp.int32),
            vmem((NB, 8, 128), jnp.int32),
            vmem((NB, 64, 8), jnp.int32),
            vmem((2, NB, 32, 256), BF16),
            vmem((2, NB, 32, 256), BF16),
            vmem((NG, 32, 256), BF16),
            vmem((NM, 32, 256), BF16),
            vmem((ROWS, 256), BF16),
            vmem((3, 256, 256), F32),
            vmem((3, 256, 256), BF16),
            vmem((3, ROWS, 256), F32),
            vmem((ROWS, 128), F32),
            vmem((ROWS, 128), F32),
            vmem((ROWS, 128), F32),
            vmem((2, ROWS, 256), BF16),
            vmem((2, NM, ROWS, 256), BF16),
            vmem((NM, ROWS, 128), BF16),
            vmem((NM, ROWS, 128), BF16),
            vmem((ROWS, 128), BF16),
            vmem((ROWS, 128), BF16),
            vmem((ROWS, 128), BF16),
            vmem((ROWS, 128), BF16),
            vmem((2, ROWS, 128), BF16),
            vmem((2, ROWS, 128), BF16),
            vmem((2, ROWS, 128), BF16),
            vmem((2, ROWS, 128), BF16),
            vmem((ROWS, 128), F32),
            vmem((ROWS, 128), BF16),
            vmem((ROWS, 128), BF16),
            pltpu.SemaphoreType.DMA((N_LOCAL,)),
            pltpu.SemaphoreType.DMA((N_REMOTE,)),
            pltpu.SemaphoreType.DMA((N_REMOTE,)),
        ],
        compiler_params=pltpu.CompilerParams(
            collective_id=0, has_side_effects=True, vmem_limit_bytes=59 * 1024 * 1024
        ),
        cost_estimate=pl.CostEstimate(
            flops=12_000_000_000, bytes_accessed=30_000_000, transcendentals=1_000_000
        ),
    )(
        hidden_in.reshape(ROWS, WIDTH),
        jnp.transpose(model_tokens, (1, 2, 0)),
        jnp.transpose(user_tokens, (1, 2, 0)),
        codebooks.reshape(1024, 256),
        decode_proj,
        conv_weight,
        conv_state,
        user_proj,
        norm_gain.reshape(32, 128),
        jnp.transpose(w_qkv, (1, 0, 2)),
        w_out,
        kv_cache,
        cache_len,
    )
    return out.reshape(64, 8, WIDTH), dec.reshape(16, 8, 128)


def solution(mesh):
    in_specs = (
        P("batch", None, None),
        P(("batch", "section"), None, None),
        P(("batch", "section"), None, None),
        P(None, "batch", None),
        P(None, "mp"),
        P(None, None, None, "mp"),
        P(("batch", "section"), None, None, None),
        P(None, ("section", "mp")),
        P(),
        P(None, None, ("section", "mp")),
        P(("section", "mp"), None),
        P(None, "batch", ("section", "mp"), None, None),
        P("batch"),
    )
    out_specs = (P("batch", None, None), P(("batch", "section"), None, "mp"))
    return jax.shard_map(
        per_device, mesh=mesh, in_specs=in_specs, out_specs=out_specs, check_vma=False
    )
```

```python
import functools
import math

import jax
import jax.numpy as jnp
from jax import lax
from jax.experimental import pallas as pl
from jax.experimental.pallas import tpu as pltpu
from jax.sharding import PartitionSpec as P

F32 = jnp.float32
BF16 = jnp.bfloat16
MESH = pl.DeviceIdType.MESH

NS, NB, NM = 4, 16, 4
NG = NS * NM
ROWS = 512
WIDTH = 4096
NCHUNK = 4
CROWS = ROWS // NCHUNK
NEG = -1e30


def dot(a, b):
    return jnp.dot(a, b, preferred_element_type=F32)


def dot_t(a, b):
    return lax.dot_general(a, b, (((1,), (1,)), ((), ())), preferred_element_type=F32)


class Sems:
    def __init__(self):
        self.used = 0

    def take(self, count=1):
        first = self.used
        self.used += count
        return first


def kernel(
    h_hbm,
    mt_hbm,
    ut_hbm,
    cb_hbm,
    dp_hbm,
    cw_hbm,
    cs_hbm,
    up_hbm,
    g_hbm,
    w_hbm,
    wo_hbm,
    kv_hbm,
    len_ref,
    outv,
    decv,
    h_v,
    tok_v,
    cb_v,
    dp_v,
    cw_v,
    cs_v,
    el_v,
    st_v,
    g32_v,
    g_v,
    w_v,
    wo_v,
    kv_v,
    upg,
    tsend,
    trecv,
    tt,
    part,
    recv,
    lg,
    lmg,
    lu,
    mq,
    mqb,
    acc,
    ss,
    cos_v,
    sin_v,
    attn_g,
    psend,
    ra_y,
    a2,
    rap,
    ram,
    ra2p,
    ra2m,
    rbp,
    rbm,
    rb2p,
    rb2m,
    b_own,
    b_y,
    rby,
    lsem,
    ssem,
    rsem,
):
    s = lax.axis_index("section")
    b = lax.axis_index("batch")
    m = lax.axis_index("mp")
    me = s * NM + m
    core = lax.rem(s, 2)
    y = s // 2
    c1 = s + 1 - 2 * core
    y1 = lax.rem(s + 2, NS)
    xp = lax.rem(m + 1, NM)
    xm = lax.rem(m + NM - 1, NM)
    xd = lax.rem(m + 2, NM)

    local = Sems()
    remote = Sems()
    finish = []

    def load(src, dst):
        copy = pltpu.make_async_copy(src, dst, lsem.at[local.take()])
        copy.start()
        return copy

    def remote_copy(src, dst, at, ds=None, db=None, dm=None):
        return pltpu.make_async_remote_copy(
            src_ref=src,
            dst_ref=dst,
            send_sem=ssem.at[at],
            recv_sem=rsem.at[at],
            device_id=(
                s if ds is None else ds,
                b if db is None else db,
                m if dm is None else dm,
            ),
            device_id_type=MESH,
        )

    def send(src, dst, **to):
        copy = remote_copy(src, dst, remote.take(), **to)
        copy.start()
        finish.append(copy.wait_send)
        return copy

    class Spread:
        def __init__(self, axis, src, dst, count=1):
            self.base = remote.take(15 * count)
            self.axis, self.src, self.dst, self.count = axis, src, dst, count
            finish.append(self.wait_send)

        def make(self, k, which):
            at = self.base + 15 * which + k - 1
            if self.axis == "batch":
                target = lax.rem(b + k, NB)
                return remote_copy(self.src(k, which), self.dst(which), at, db=target)
            target = lax.rem(me + k, NG)
            return remote_copy(
                self.src(k, which),
                self.dst(which),
                at,
                ds=target // NM,
                dm=lax.rem(target, NM),
            )

        def start(self, which=0):
            @pl.loop(1, 16)
            def _(k):
                self.make(k, which).start()

        def wait_recv(self, which=0):
            @pl.loop(1, 16)
            def _(k):
                self.make(k, which).wait_recv()

        def wait_send(self):
            for which in range(self.count):

                @pl.loop(1, 16)
                def _(k):
                    self.make(k, which).wait_send()

    class Event:
        def __init__(self, src, dst, count=NCHUNK, **to):
            self.base = remote.take(count)
            self.src, self.dst, self.to, self.count = src, dst, to, count
            finish.append(self.wait_sends)

        def make(self, c):
            return remote_copy(self.src(c), self.dst(c), self.base + c, **self.to)

        def start(self, c):
            self.make(c).start()

        def wait(self, c):
            self.make(c).wait_recv()

        def wait_sends(self):
            @pl.loop(0, self.count)
            def _(c):
                self.make(c).wait_send()

    barrier = pltpu.get_barrier_semaphore()

    @pl.loop(1, 16)
    def _(k):
        pl.semaphore_signal(
            barrier, inc=1, device_id=(s, lax.rem(b + k, NB), m), device_id_type=MESH
        )
        other = lax.rem(me + k, NG)
        pl.semaphore_signal(
            barrier, inc=1, device_id=(other // NM, b, lax.rem(other, NM)), device_id_type=MESH
        )

    l_ut = load(ut_hbm, tok_v.at[0])
    l_mt = load(mt_hbm, tok_v.at[1])
    l_up = load(up_hbm, upg.at[me])
    l_cb = load(cb_hbm, cb_v)
    l_g = load(g_hbm, g32_v)
    l_h = load(h_hbm, h_v)
    l_w = load(w_hbm, w_v)
    l_wo = []
    for yy in range(2):
        cols = pl.ds(pl.multiple_of((2 * yy + core) * 1024, 1024), 1024)
        l_wo.append(load(wo_hbm.at[:, cols], wo_v.at[core, yy]))
    l_cs = load(cs_hbm, cs_v)
    l_kv = load(kv_hbm, kv_v)
    l_dp = load(dp_hbm, dp_v)
    l_cw = load(cw_hbm, cw_v)

    l_ut.wait()
    l_mt.wait()
    f0 = 2 * m
    tile = jnp.concatenate(
        [
            tok_v[0, f0],
            tok_v[0, f0 + 1],
            tok_v[1, f0],
            tok_v[1, f0 + 1],
            jnp.zeros((8, 64), jnp.int32),
        ],
        axis=1,
    )
    tsend[...] = tile
    trecv[b] = tile
    pl.semaphore_wait(barrier, 30)
    tok = Spread("batch", lambda k, w: tsend, lambda w: trecv.at[b])
    tok.start()

    def up_send(block, **to):
        return send(upg.at[block], upg.at[block], **to)

    l_up.wait()
    u_y = up_send(me, ds=y1)
    u_p = up_send(me, dm=xp)
    u_m = up_send(me, dm=xm)
    wo_copies = []
    for yy in range(2):
        cols = pl.ds(pl.multiple_of((2 * yy + 1 - core) * 1024, 1024), 1024)
        wo_copies.append(send(wo_hbm.at[:, cols], wo_v.at[core, yy], ds=c1))

    lane = lax.broadcasted_iota(jnp.int32, (64, 128), 1)
    freq = jnp.exp(lax.rem(lane, 64).astype(F32) * (-2.0 * math.log(10000.0) / 128.0))
    frame = lax.rem(lax.broadcasted_iota(jnp.int32, (64, 128), 0), 8)

    @pl.loop(0, 8)
    def _(i):
        where = lax.broadcasted_iota(jnp.int32, (64, 128), 0) // 8
        pos = frame
        for d in range(8):
            pos = pos + jnp.where(where == d, len_ref[i * 8 + d], 0)
        angle = pos.astype(F32) * freq
        rows = pl.ds(pl.multiple_of(i * 64, 64), 64)
        cos_v[rows] = jnp.cos(angle)
        sine = jnp.sin(angle)
        sin_v[rows] = jnp.where(lane < 64, -sine, sine)

    l_g.wait()
    gain = g32_v[...].astype(F32)
    for i in range(32):
        g_v[:, pl.ds(128 * i, 128)] = gain[i : i + 1]

    u_y.wait_recv()
    yblk = y1 * NM + m
    u_yp = up_send(yblk, dm=xp)
    u_ym = up_send(yblk, dm=xm)

    tok.wait_recv()
    l_cb.wait()

    @pl.loop(0, NB)
    def _(k):
        tt[k] = trecv[lax.rem(b + k, NB)].T[:64]

    entry = lax.broadcasted_iota(jnp.int32, (128, 128), 1) + 128 * b
    pieces = Spread("batch", lambda k, w: part.at[w, k], lambda w: recv.at[w, b], 2)

    def look_up(which):
        @pl.loop(0, 4)
        def _(quad):
            rows = tt[pl.ds(4 * quad, 4), pl.ds(32 * which, 32), :].reshape(128, 8)
            hot = [jnp.where(rows[:, c : c + 1] == entry, 1.0, 0.0).astype(BF16) for c in range(8)]
            piece = dot(jnp.concatenate(hot, axis=1), cb_v[...])
            part[which, pl.ds(4 * quad, 4)] = piece.astype(BF16).reshape(4, 32, 256)

            if which == 0:

                @pl.loop(0, 4)
                def _(j):
                    k = 4 * quad + j

                    @pl.when(k > 0)
                    def _():
                        pieces.make(k, which).start()

        recv[which, b] = part[which, 0]

    look_up(0)

    u_p.wait_recv()
    u_f = up_send(s * NM + xm, dm=xp)
    u_m.wait_recv()
    u_yp.wait_recv()
    u_ym.wait_recv()
    u_yf = up_send(y1 * NM + xp, dm=xm)

    l_cs.wait()

    @pl.loop(0, 4)
    def _(layer):
        rows = [cs_v[d, layer].astype(F32) for d in range(16)]
        for j in range(2):
            el_v[layer, pl.ds(16 * j, 16), :] = jnp.concatenate(
                [row[j : j + 1] for row in rows], axis=0
            ).astype(BF16)

    l_h.wait()
    l_w.wait()
    acc[...] = jnp.zeros_like(acc)

    @pl.loop(0, 4)
    def _(step):
        cols = pl.ds(pl.multiple_of(step * 1024, 1024), 1024)
        scaled = (h_v[:, cols].astype(F32) * g_v[:, cols]).astype(BF16)
        for j in range(3):
            acc[j] += dot(scaled, w_v[j, cols, :])

    look_up(1)

    u_f.wait_recv()
    u_yf.wait_recv()
    mine = pl.ds(pl.multiple_of(s * NM, NM), NM)
    yours = pl.ds(pl.multiple_of(y1 * NM, NM), NM)
    u_c = [up_send(mine, ds=c1), up_send(yours, ds=c1)]

    def total_of(which):
        def step(i, total):
            return total + recv[which, i].astype(F32)

        return lax.fori_loop(0, NB, step, jnp.zeros((32, 256), F32)).astype(BF16)

    pieces.wait_recv(0)
    lg[me] = total_of(0)
    latents = Spread("group", lambda k, w: lg.at[me], lambda w: lg.at[me])
    latents.start()
    pieces.start(1)

    mq[...] = jnp.zeros_like(mq)
    for copy in u_c:
        copy.wait_recv()

    @pl.loop(0, NS)
    def _(j):
        cols = pl.ds(pl.multiple_of(j * 1024, 1024), 1024)
        wide_up = jnp.concatenate([upg[NM * j + i] for i in range(NM)], axis=1)
        scaled = (wide_up.astype(F32) * g_v[:, cols]).astype(BF16)
        for t in range(3):
            mq[t] += dot(scaled, w_v[t, cols, :])

    mqb[...] = mq[...].astype(BF16)

    latents.wait_recv()
    to = lax.broadcasted_iota(jnp.int32, (128, 128), 0)
    frm = lax.broadcasted_iota(jnp.int32, (128, 128), 1)
    perm = jnp.where(frm == lax.rem(to, 8) * 16 + to // 8, 1.0, 0.0).astype(BF16)

    @pl.loop(0, NS)
    def _(i):
        group = lg[pl.ds(NM * i, NM)].reshape(128, 256)
        lu[pl.ds(pl.multiple_of(128 * i, 128), 128)] = dot(perm, group).astype(BF16)

    ss[...] = jnp.zeros_like(ss)

    @pl.loop(0, NG, unroll=2)
    def _(j):
        cols = pl.ds(pl.multiple_of(j * 256, 256), 256)
        x0 = h_v[:, cols].astype(F32) + dot(lu[...], upg[j])
        sq = x0 * x0
        ss[...] += sq[:, :128] + sq[:, 128:]

    l_kv.wait()
    for copy in l_wo:
        copy.wait()
    for copy in wo_copies:
        copy.wait_recv()
    l_dp.wait()
    l_cw.wait()

    my_cols = pl.ds(pl.multiple_of(me * 256, 256), 256)
    row8 = lax.broadcasted_iota(jnp.int32, (32, 32), 0)
    col8 = lax.broadcasted_iota(jnp.int32, (32, 32), 1)
    new_ok = (row8 // 8 == col8 // 8) & (lax.rem(col8, 8) <= lax.rem(row8, 8))
    slot = lax.broadcasted_iota(jnp.int32, (8, 256), 1)

    def span(c, lower=0, count=CROWS):
        start = pl.multiple_of(c * CROWS + lower, CROWS // 2)
        return pl.ds(start, count)

    half = CROWS // 2

    def lo(c):
        return span(c, 0, half)

    def hi(c):
        return span(c, half, half)

    def attention(c):
        rows = span(c)
        r = lax.rsqrt(jnp.sum(ss[rows], axis=-1, keepdims=True) * (1.0 / WIDTH) + 1e-05)
        lat = lu[rows]
        q, k, v = [(acc[t, rows] + dot(lat, mqb[t])) * r for t in range(3)]
        cosine, sine = cos_v[rows], sin_v[rows]

        def rope(z):
            return (z * cosine + pltpu.roll(z, 64, 1) * sine).astype(BF16)

        for hd in range(2):
            cut = slice(128 * hd, 128 * hd + 128)
            qh, kh, vh = rope(q[:, cut]), rope(k[:, cut]), v[:, cut].astype(BF16)
            pieces = []
            for i in range(CROWS // 32):
                d0 = c * (CROWS // 8) + 4 * i
                sub = slice(32 * i, 32 * i + 32)
                keys = kv_v[0, pl.ds(d0, 4), hd].reshape(256, 128)
                values = kv_v[1, pl.ds(d0, 4), hd].reshape(256, 128)
                old = dot_t(qh[sub], keys) * (1.0 / math.sqrt(128.0))
                parts = []
                for d in range(4):
                    ok = (slot >= 64 * d) & (slot < 64 * d + len_ref[d0 + d])
                    parts.append(jnp.where(ok, old[8 * d : 8 * d + 8], NEG))
                old = jnp.concatenate(parts, axis=0)
                new = dot_t(qh[sub], kh[sub]) * (1.0 / math.sqrt(128.0))
                new = jnp.where(new_ok, new, NEG)
                top = jnp.maximum(
                    jnp.max(old, axis=-1, keepdims=True), jnp.max(new, axis=-1, keepdims=True)
                )
                old = jnp.exp(old - top)
                new = jnp.exp(new - top)
                total = jnp.sum(old, axis=-1, keepdims=True) + jnp.sum(
                    new, axis=-1, keepdims=True
                )
                mixed = dot(old.astype(BF16), values) + dot(new.astype(BF16), vh[sub])
                pieces.append((mixed / total).astype(BF16))
            attn_g[core, rows, pl.ds(128 * hd, 128)] = jnp.concatenate(pieces, axis=0)

    e_t = Event(lambda c: attn_g.at[core, span(c)], lambda c: attn_g.at[core, span(c)], ds=c1)
    lane_a, lane_b = pl.ds(0, 128), pl.ds(128, 128)
    e_ay = Event(lambda c: psend.at[1 - y, :, span(c), lane_a], lambda c: ra_y.at[:, span(c)], ds=y1)
    e_bp = Event(lambda c: psend.at[:, xd, lo(c), lane_b], lambda c: rbp.at[:, lo(c)], dm=xp)
    e_bm = Event(lambda c: psend.at[:, xd, hi(c), lane_b], lambda c: rbm.at[:, hi(c)], dm=xm)
    e_ap = Event(lambda c: a2.at[xd, lo(c)], lambda c: rap.at[lo(c)], dm=xp)
    e_am = Event(lambda c: a2.at[xd, hi(c)], lambda c: ram.at[hi(c)], dm=xm)
    e_bp2 = Event(lambda c: psend.at[:, xp, span(c), lane_b], lambda c: rb2p.at[:, span(c)], dm=xp)
    e_bm2 = Event(lambda c: psend.at[:, xm, span(c), lane_b], lambda c: rb2m.at[:, span(c)], dm=xm)
    e_ap2 = Event(lambda c: a2.at[xp, span(c)], lambda c: ra2p.at[span(c)], dm=xp)
    e_am2 = Event(lambda c: a2.at[xm, span(c)], lambda c: ra2m.at[span(c)], dm=xm)
    e_by = Event(lambda c: b_y.at[span(c)], lambda c: rby.at[span(c)], ds=y1)

    def gather(owner, first, count, **to):
        def at(c):
            start = pl.multiple_of(owner * 256 + first, 128)
            return outv.at[span(c), pl.ds(start, count)]

        return Event(at, at, **to)

    g_p = gather(me, 0, 256, dm=xp)
    g_m = gather(me, 0, 256, dm=xm)
    g_y = gather(me, 0, 256, ds=y1)
    g_ap = gather(y1 * NM + m, 0, 128, dm=xp)
    g_am = gather(y1 * NM + m, 0, 128, dm=xm)
    g_pp = gather(s * NM + xm, 0, 128, dm=xp)
    g_mm = gather(s * NM + xp, 128, 128, dm=xm)
    g_bm = gather(s * NM + xm, 128, 128, ds=y1)
    g_bp = gather(s * NM + xp, 128, 128, ds=y1)
    g_ad = gather(y1 * NM + xm, 0, 128, dm=xp)
    g_bd = gather(s * NM + xd, 128, 128, ds=y1)
    g_f1 = gather(s * NM, 0, 1024, ds=c1)
    g_f2 = gather(y1 * NM, 0, 1024, ds=c1)

    def stage_a(c):
        attention(c)
        e_t.start(c)

    def stage_o(c):
        e_t.wait(c)
        rows = span(c)
        for yy in range(2):
            proj = dot(attn_g[0, rows], wo_v[0, yy]) + dot(attn_g[1, rows], wo_v[1, yy])
            for t in range(NM):
                psend[yy, t, rows] = proj[:, 256 * t : 256 * t + 256].astype(BF16)
        e_ay.start(c)
        e_bp.start(c)
        e_bm.start(c)

    def add(place, other):
        place[...] = (place[...].astype(F32) + other.astype(F32)).astype(BF16)

    def stage_p(c):
        rows = span(c)
        e_bp.wait(c)
        add(psend.at[:, xp, lo(c), lane_b], rbp[:, lo(c)])
        e_bp2.start(c)
        e_bm.wait(c)
        add(psend.at[:, xm, hi(c), lane_b], rbm[:, hi(c)])
        e_bm2.start(c)
        e_ay.wait(c)
        a2[:, rows] = (
            psend[y, :, rows, lane_a].astype(F32) + ra_y[:, rows].astype(F32)
        ).astype(BF16)
        e_ap.start(c)
        e_am.start(c)

    def stage_q(c):
        rows = span(c)
        e_ap.wait(c)
        add(a2.at[xp, lo(c)], rap[lo(c)])
        e_ap2.start(c)
        e_am.wait(c)
        add(a2.at[xm, hi(c)], ram[hi(c)])
        e_am2.start(c)
        e_bp2.wait(c)
        e_bm2.wait(c)

        def total(yy):
            ours = psend[yy, m, rows, lane_b].astype(F32)
            return ours + rb2p[yy, rows].astype(F32) + rb2m[yy, rows].astype(F32)

        b_y[rows] = total(1 - y).astype(BF16)
        e_by.start(c)
        b_own[rows] = total(y)

    def stage_r(c):
        rows = span(c)
        x0 = h_v[rows, my_cols].astype(F32) + dot(lu[rows], upg[me])
        e_ap2.wait(c)
        e_am2.wait(c)
        first = a2[m, rows].astype(F32) + ra2p[rows].astype(F32) + ra2m[rows].astype(F32)
        e_by.wait(c)
        second = b_own[rows] + rby[rows].astype(F32)
        total = jnp.concatenate([first, second], axis=1)
        outv[rows, my_cols] = (x0 + total).astype(BF16)
        for event in (g_y, g_p, g_m):
            event.start(c)

    def stage_g(c):
        g_y.wait(c)
        g_ap.start(c)
        g_am.start(c)
        g_p.wait(c)
        g_pp.start(c)
        g_bm.start(c)
        g_m.wait(c)
        g_mm.start(c)
        g_bp.start(c)

    def stage_h(c):
        g_ap.wait(c)
        g_ad.start(c)
        g_mm.wait(c)
        g_bd.start(c)
        g_pp.wait(c)
        g_f1.start(c)

    def stage_i(c):
        for event in (g_am, g_bm, g_bp, g_ad, g_bd):
            event.wait(c)
        g_f2.start(c)

    def stage_j(c):
        g_f1.wait(c)
        g_f2.wait(c)

    def excite(layer, state):
        excited = jnp.where(state > 0, state, jnp.exp(jnp.minimum(state, 0.0)) - 1.0)
        place = el_v.at[layer, pl.ds(32, 128), pl.ds(pl.multiple_of(m * 128, 128), 128)]
        place[...] = excited.astype(BF16)
        st_v[...] = state

    def codec_at(layer):
        return el_v.at[layer, pl.ds(32, 128), pl.ds(pl.multiple_of(m * 128, 128), 128)]

    codec_moves = [Event(codec_at, codec_at, 4, dm=t) for t in (xp, xm, xd)]

    lm_moves = [Event(lambda c: lmg.at[m], lambda c: lmg.at[m], 1, dm=t) for t in (xp, xm, xd)]

    def codec_latents():
        pieces.wait_recv(1)
        lmg[m] = total_of(1)
        for move in lm_moves:
            move.start(0)

    def codec_start():
        for move in lm_moves:
            move.wait(0)
        excite(0, dot(lmg[...].reshape(128, 256), dp_v[...]))
        for move in codec_moves:
            move.start(0)

    def codec_step(layer):
        for move in codec_moves:
            move.wait(layer)
        state = st_v[...]
        for tap in range(3):
            state = state + dot(el_v[layer, pl.ds(16 * tap, 128), :], cw_v[layer, tap])
        st_v[...] = state

        @pl.when(layer < 3)
        def _():
            excite(layer + 1, state)
            for move in codec_moves:
                move.start(layer + 1)

    stages = [stage_o, stage_p, stage_q, stage_r, stage_g, stage_h, stage_i, stage_j]

    @pl.loop(0, NCHUNK + len(stages))
    def _(step):
        pl.when(step < NCHUNK)(lambda: stage_a(step))
        for place, stage in enumerate(stages):
            c = step - 1 - place

            @pl.when((c >= 0) & (c < NCHUNK))
            def _():
                stage(c)

        pl.when(step == 1)(codec_latents)
        pl.when(step == 2)(codec_start)

        @pl.when((step >= 3) & (step < 7))
        def _():
            codec_step(step - 3)

    decv[...] = dot(perm, st_v[...].astype(BF16)).astype(BF16)
    for done in finish:
        done()


N_LOCAL = 16
N_REMOTE = 256


def per_device(
    hidden_in,
    model_tokens,
    user_tokens,
    codebooks,
    decode_proj,
    conv_weight,
    conv_state,
    user_proj,
    norm_gain,
    w_qkv,
    w_out,
    kv_cache,
    cache_len,
):
    any_space = pl.BlockSpec(memory_space=pl.ANY)
    smem = pl.BlockSpec(memory_space=pltpu.SMEM)
    vmem = pltpu.VMEM
    out, dec = pl.pallas_call(
        kernel,
        out_shape=(vmem((ROWS, WIDTH), BF16), vmem((128, 128), BF16)),
        in_specs=[any_space] * 12 + [smem],
        out_specs=(pl.BlockSpec(memory_space=vmem), pl.BlockSpec(memory_space=vmem)),
        scratch_shapes=[
            vmem((ROWS, WIDTH), BF16),
            vmem((2, 8, 8, 16), jnp.int32),
            vmem((1024, 256), BF16),
            vmem((256, 128), BF16),
            vmem((4, 3, 512, 128), BF16),
            vmem((16, 4, 2, 512), BF16),
            vmem((4, 160, 512), BF16),
            vmem((128, 128), F32),
            vmem((32, 128), BF16),
            vmem((1, WIDTH), F32),
            vmem((3, WIDTH, 256), BF16),
            vmem((2, 2, 256, 1024), BF16),
            vmem((2, 64, 2, 64, 128), BF16),
            vmem((NG, 256, 256), BF16),
            vmem((8, 128), jnp.int32),
            vmem((NB, 8, 128), jnp.int32),
            vmem((NB, 64, 8), jnp.int32),
            vmem((2, NB, 32, 256), BF16),
            vmem((2, NB, 32, 256), BF16),
            vmem((NG, 32, 256), BF16),
            vmem((NM, 32, 256), BF16),
            vmem((ROWS, 256), BF16),
            vmem((3, 256, 256), F32),
            vmem((3, 256, 256), BF16),
            vmem((3, ROWS, 256), F32),
            vmem((ROWS, 128), F32),
            vmem((ROWS, 128), F32),
            vmem((ROWS, 128), F32),
            vmem((2, ROWS, 256), BF16),
            vmem((2, NM, ROWS, 256), BF16),
            vmem((NM, ROWS, 128), BF16),
            vmem((NM, ROWS, 128), BF16),
            vmem((ROWS, 128), BF16),
            vmem((ROWS, 128), BF16),
            vmem((ROWS, 128), BF16),
            vmem((ROWS, 128), BF16),
            vmem((2, ROWS, 128), BF16),
            vmem((2, ROWS, 128), BF16),
            vmem((2, ROWS, 128), BF16),
            vmem((2, ROWS, 128), BF16),
            vmem((ROWS, 128), F32),
            vmem((ROWS, 128), BF16),
            vmem((ROWS, 128), BF16),
            pltpu.SemaphoreType.DMA((N_LOCAL,)),
            pltpu.SemaphoreType.DMA((N_REMOTE,)),
            pltpu.SemaphoreType.DMA((N_REMOTE,)),
        ],
        compiler_params=pltpu.CompilerParams(
            collective_id=0, has_side_effects=True, vmem_limit_bytes=59 * 1024 * 1024
        ),
        cost_estimate=pl.CostEstimate(
            flops=12_000_000_000, bytes_accessed=30_000_000, transcendentals=1_000_000
        ),
    )(
        hidden_in.reshape(ROWS, WIDTH),
        jnp.transpose(model_tokens, (1, 2, 0)),
        jnp.transpose(user_tokens, (1, 2, 0)),
        codebooks.reshape(1024, 256),
        decode_proj,
        conv_weight,
        conv_state,
        user_proj,
        norm_gain.reshape(32, 128),
        jnp.transpose(w_qkv, (1, 0, 2)),
        w_out,
        kv_cache,
        cache_len,
    )
    return out.reshape(64, 8, WIDTH), dec.reshape(16, 8, 128)


def solution(mesh):
    in_specs = (
        P("batch", None, None),
        P(("batch", "section"), None, None),
        P(("batch", "section"), None, None),
        P(None, "batch", None),
        P(None, "mp"),
        P(None, None, None, "mp"),
        P(("batch", "section"), None, None, None),
        P(None, ("section", "mp")),
        P(),
        P(None, None, ("section", "mp")),
        P(("section", "mp"), None),
        P(None, "batch", ("section", "mp"), None, None),
        P("batch"),
    )
    out_specs = (P("batch", None, None), P(("batch", "section"), None, "mp"))
    return jax.shard_map(
        per_device, mesh=mesh, in_specs=in_specs, out_specs=out_specs, check_vma=False
    )
```
